512 devices in a mesh: ctx: 128 (over y, z, core), head: 4 (over x).
Axes of the slice: x: 4, y: 8, z: 8, core: 2. Of those that a mesh axis runs over, the one named last changes fastest.
Arguments:
- queries: bfloat16 [65536, 32, 128], P(('ctx', 'head')), may hold values from -6 to 6
- key_states: bfloat16 [65536, 4, 128], P(('ctx', 'head')), may hold values from -6 to 6
- value_states: bfloat16 [65536, 4, 128], P(('ctx', 'head')), may hold values from -6 to 6
- out_grad: bfloat16 [65536, 32, 128], P(('ctx', 'head')), may hold values from -6 to 6
- log_sums: float32 [32, 65536], P('head', 'ctx'), may hold values from 3 to 6
- row_deltas: float32 [32, 65536], P('head', 'ctx'), may hold values from -10 to 10
- block_pairs: int32 [1024, 4], replicated, may hold values from 0 to 1023, as said below
- pair_kinds: int32 [1024, 4], replicated, may hold values from 0 to 2, as said below
Outputs:
- query_grad: bfloat16 [65536, 32, 128], P(('ctx', 'head'))
- key_grad: bfloat16 [65536, 4, 128], P(('ctx', 'head'))
- value_grad: bfloat16 [65536, 4, 128], P(('ctx', 'head'))
The draws below stay inside these ranges and needn't reach their ends.
Inputs may be any that keep to these rules, and one draw needn't show every extreme that they name: `block_pairs`: row g lists the key blocks of query block g. Slot 0 names g itself, slot 1 names g - 1, slot 2 names key block 0; slots 3 and up name blocks of shards at least two shards before the shard of g, never of shard 0. The blocks of the live slots of a row are distinct and none is later than g; a slot of kind 0 names block 0. Counting shards of 8 consecutive query blocks, the query blocks of one shard name at most one key block held by any other single shard, and this is reached. `pair_kinds`: 1 marks a full block pair, 2 the pair of a block with itself, 0 an unused slot. Slot 0 is always 2 and no other slot is 2; slot 1 is 0 only for g = 0; slot 2 is 0 exactly for g < 2 and for the query blocks of the second shard.
All inputs are finite; a program needn't handle non-finite values.
Results may differ from the reference program's by a relative error of at most 0.0012.
The reference program's roundings to bfloat16 on the way count: a program that leaves them out, or rounds other values in their place, can miss the bound.
Values may be sent and summed in bfloat16 or wider, within the bound.
No kernel may reach another device: no remote copies, remote signals or barrier semaphores. Data moves between devices by JAX's collectives and lax.ppermute only.
A program may use at most 64 MiB of HBM per device.

```python
import jax
import jax.numpy as jnp
from jax import lax

HD = 128
QH = 32
KVH = 4
BLOCK = 64
REMOTE = 1
TOKENS = 65536
QB_DEV = 8
NQB = 1024


def pair_table(key):
    base_key = jax.random.fold_in(key, 4711)
    shards = NQB // QB_DEV
    spread = QB_DEV * REMOTE
    pool = max(spread, shards)
    order_keys = jax.random.split(jax.random.fold_in(base_key, 1), shards)
    orders = jax.vmap(lambda sub_key: jax.random.permutation(sub_key, pool)[:spread])(order_keys).astype(jnp.int32)
    links = jax.random.randint(jax.random.fold_in(base_key, 2), (shards, shards), 0, QB_DEV).astype(jnp.int32)
    dropped = jax.random.randint(jax.random.fold_in(base_key, 3), (shards, spread), 0, 4)
    shard_ids = jnp.arange(shards, dtype=jnp.int32)[:, None]
    owners = jnp.minimum(orders, shards - 1).astype(jnp.int32)
    is_live = (orders >= 1) & (orders <= shard_ids - 2) & (dropped > 0)
    chosen = jnp.take_along_axis(links, owners, axis=1)
    far_blocks = jnp.where(is_live, owners * QB_DEV + chosen, 0).astype(jnp.int32).reshape(NQB, REMOTE)
    far_kinds = is_live.astype(jnp.int32).reshape(NQB, REMOTE)
    query_ids = jnp.arange(NQB, dtype=jnp.int32)
    shard_of = query_ids // QB_DEV
    prev_kind = (query_ids >= 1).astype(jnp.int32)
    hub_kind = ((query_ids >= 2) & (shard_of != 1)).astype(jnp.int32)
    near_blocks = jnp.stack([query_ids, jnp.where(prev_kind > 0, query_ids - 1, 0), jnp.zeros_like(query_ids)], axis=1)
    near_kinds = jnp.stack([jnp.full_like(query_ids, 2), prev_kind, hub_kind], axis=1)
    blocks_all = jnp.concatenate([near_blocks, far_blocks], axis=1).astype(jnp.int32)
    kinds_all = jnp.concatenate([near_kinds, far_kinds], axis=1).astype(jnp.int32)
    return (blocks_all, kinds_all)


def draw_block_pairs(key, part):
    return pair_table(key)[0]


def draw_pair_kinds(key, part):
    return pair_table(key)[1]


def block_levels(own_key, shape, cuts, smallest, top_value):
    level = 1.0
    for position, parts in cuts:
        draws = jax.random.uniform(jax.random.fold_in(jax.random.fold_in(own_key, 6), position), (parts,), jnp.float32, smallest / len(cuts), top_value / len(cuts))
        level = level * jnp.repeat(jnp.exp(draws), shape[position] // parts).reshape((-1,) + (1,) * (len(shape) - 1 - position))
    return level


def bell_draw(stream_key, extent, width, limit, cuts=(), held_as=jnp.bfloat16):
    result = width * jax.random.normal(stream_key, extent, jnp.float32)
    if cuts:
        result = result * block_levels(stream_key, extent, cuts, -0.22, 0.18)
    return jnp.clip(result, -limit, limit).astype(held_as)


def setup_inputs(seed: int = 0) -> dict:
    key_list = jax.random.split(jax.random.key(seed), 9)
    queries = bell_draw(key_list[0], (TOKENS, QH, HD), 1.0, 6.0, ((0, 512),))
    key_states = bell_draw(key_list[1], (TOKENS, KVH, HD), 1.0, 6.0, ((0, 512),))
    value_states = bell_draw(key_list[2], (TOKENS, KVH, HD), 1.0, 6.0, ((0, 512),))
    out_grad = bell_draw(key_list[3], (TOKENS, QH, HD), 1.0, 6.0, ((0, 512),))
    log_sums = jnp.clip(3.0 + 3.0 * jax.random.uniform(key_list[4], (QH, TOKENS), jnp.float32) ** block_levels(key_list[4], (QH, TOKENS), ((0, 4), (1, 128)), -0.2, 0.2), 3.0, 6.0)
    row_deltas = bell_draw(key_list[5], (QH, TOKENS), 2.0, 10.0, ((0, 4), (1, 128)), jnp.float32)
    block_pairs = draw_block_pairs(jax.random.fold_in(key_list[8], 71), 0)
    pair_kinds = draw_pair_kinds(jax.random.fold_in(key_list[8], 71), 0)
    return {"queries": queries, "key_states": key_states, "value_states": value_states, "out_grad": out_grad, "log_sums": log_sums, "row_deltas": row_deltas, "block_pairs": block_pairs, "pair_kinds": pair_kinds}


def reference(queries, key_states, value_states, out_grad, log_sums, row_deltas, block_pairs, pair_kinds):
    head_group = QH // KVH
    score_scale = HD ** -0.5
    causal = jnp.arange(BLOCK)[:, None] >= jnp.arange(BLOCK)[None, :]
    query_all = queries.astype(jnp.float32).reshape(NQB, BLOCK, KVH, head_group, HD).transpose(2, 0, 1, 3, 4)
    grad_all = out_grad.astype(jnp.float32).reshape(NQB, BLOCK, KVH, head_group, HD).transpose(2, 0, 1, 3, 4)
    key_all = key_states.astype(jnp.float32).reshape(NQB, BLOCK, KVH, HD).transpose(2, 0, 1, 3)
    value_all = value_states.astype(jnp.float32).reshape(NQB, BLOCK, KVH, HD).transpose(2, 0, 1, 3)
    log_all = log_sums.reshape(KVH, head_group, NQB, BLOCK).transpose(0, 2, 1, 3)
    delta_all = row_deltas.reshape(KVH, head_group, NQB, BLOCK).transpose(0, 2, 1, 3)

    def per_head(inputs):
        head_queries, head_grads, head_keys, head_values, head_logs, head_deltas = inputs

        def per_slot(running, column):
            query_acc, key_acc, value_acc = running
            slot_blocks, slot_kinds = column
            key_tile = head_keys[slot_blocks]
            value_tile = head_values[slot_blocks]
            scores = jnp.einsum("nbgd,nkd->ngbk", head_queries, key_tile) * score_scale
            weights = jnp.exp(scores - head_logs[..., None])
            full_pair = (slot_kinds == 1)[:, None, None, None]
            diagonal_pair = (slot_kinds == 2)[:, None, None, None]
            weights = jnp.where(full_pair | (diagonal_pair & causal), weights, 0.0)
            rounded = lax.optimization_barrier(weights.astype(jnp.bfloat16)).astype(jnp.float32)
            value_term = jnp.einsum("ngbk,nbgd->nkd", rounded, head_grads)
            prob_grad = jnp.einsum("nbgd,nkd->ngbk", head_grads, value_tile)
            dscore = weights * (prob_grad - head_deltas[..., None])
            dscore = lax.optimization_barrier(dscore.astype(jnp.bfloat16)).astype(jnp.float32)
            query_acc = query_acc + jnp.einsum("ngbk,nkd->nbgd", dscore, key_tile) * score_scale
            key_term = jnp.einsum("ngbk,nbgd->nkd", dscore, head_queries) * score_scale
            key_acc = key_acc.at[slot_blocks].add(key_term)
            value_acc = value_acc.at[slot_blocks].add(value_term)
            return (query_acc, key_acc, value_acc), None

        initial = (jnp.zeros((NQB, BLOCK, head_group, HD), jnp.float32),
                   jnp.zeros((NQB, BLOCK, HD), jnp.float32),
                   jnp.zeros((NQB, BLOCK, HD), jnp.float32))
        finals, unused = lax.scan(per_slot, initial, (block_pairs.T, pair_kinds.T))
        return finals

    query_acc, key_acc, value_acc = lax.map(per_head, (query_all, grad_all, key_all, value_all, log_all, delta_all))
    query_grad = query_acc.transpose(1, 2, 0, 3, 4).reshape(TOKENS, QH, HD).astype(jnp.bfloat16)
    key_grad = key_acc.transpose(1, 2, 0, 3).reshape(TOKENS, KVH, HD).astype(jnp.bfloat16)
    value_grad = value_acc.transpose(1, 2, 0, 3).reshape(TOKENS, KVH, HD).astype(jnp.bfloat16)
    return query_grad, key_grad, value_grad
```

```python
import jax
import jax.numpy as jnp
from jax import lax
from jax.experimental import pallas as pl
from jax.experimental.pallas import tpu as pltpu
from jax.sharding import PartitionSpec as P

BLOCK = 64
WIDTH = 128
AXES = ("ctx", "head")
VMEM_BYTES = 48 * 1024 * 1024


def dot(left, right, contract):
    return lax.dot_general(
        left, right, (contract, ((), ())), preferred_element_type=jnp.float32
    )


def attend(kinds, q_ref, g_ref, own_ref, got_ref, log_ref, delta_ref, dq_ref, down_ref, dprev_ref, dfar_ref):
    group = q_ref.shape[1]
    rows = BLOCK * group
    scale = WIDTH ** (-0.5)
    key_at = lax.broadcasted_iota(jnp.int32, (BLOCK, rows), 0)
    token_at = lax.broadcasted_iota(jnp.int32, (BLOCK, rows), 1) // group
    causal = key_at <= token_at
    terms = []
    for blk in range(2):
        mine = slice(blk * BLOCK, (blk + 1) * BLOCK)
        tables = []
        for kv in range(2):
            before = own_ref[kv, 0, :BLOCK] if blk else got_ref[3, kv, 0]
            tables.append(
                jnp.concatenate(
                    [own_ref[kv, 0, mine], before, got_ref[2, kv, 0], got_ref[blk, kv, 0]], axis=0
                )
            )
        keys, values = tables
        queries = q_ref[mine].reshape(rows, WIDTH)
        grads = g_ref[mine].reshape(rows, WIDTH)
        scores = dot(keys, queries, ((1,), (1,))) * scale
        weights = jnp.exp(scores - log_ref[blk, 0])
        parts = [jnp.where(causal, weights[:BLOCK], 0.0)]
        for slot in range(1, 4):
            live = kinds[blk, slot] > 0
            parts.append(jnp.where(live, weights[slot * BLOCK : (slot + 1) * BLOCK], 0.0))
        weights = jnp.concatenate(parts, axis=0)
        prob_grad = dot(values, grads, ((1,), (1,)))
        dscore = (weights * (prob_grad - delta_ref[blk, 0])).astype(jnp.bfloat16)
        dvalue = dot(weights.astype(jnp.bfloat16), grads, ((1,), (0,)))
        dkey = dot(dscore, queries, ((1,), (0,))) * scale
        dquery = dot(dscore, keys, ((0,), (0,))) * scale
        dq_ref[mine] = dquery.reshape(BLOCK, group, WIDTH).astype(dq_ref.dtype)
        terms.append((dkey, dvalue))
    for kv in range(2):
        first, second = terms[0][kv], terms[1][kv]
        down_ref[kv, 0, :BLOCK] = first[:BLOCK] + second[BLOCK : 2 * BLOCK]
        down_ref[kv, 0, BLOCK:] = second[:BLOCK]
        dprev_ref[kv, 0] = first[BLOCK : 2 * BLOCK]
        dfar_ref[0, kv, 0] = first[3 * BLOCK :]
        dfar_ref[1, kv, 0] = second[3 * BLOCK :]
        dfar_ref[2, kv, 0] = first[2 * BLOCK : 3 * BLOCK] + second[2 * BLOCK : 3 * BLOCK]


def attention(kinds, queries, grads, own, got, logs, deltas):
    tokens, heads, _ = queries.shape
    key_heads = own.shape[1]
    group = heads // key_heads
    token_spec = pl.BlockSpec((tokens, group, WIDTH), lambda k: (0, k, 0))
    own_spec = pl.BlockSpec((2, 1, tokens, WIDTH), lambda k: (0, k, 0, 0))
    got_spec = pl.BlockSpec((4, 2, 1, BLOCK, WIDTH), lambda k: (0, 0, k, 0, 0))
    stat_spec = pl.BlockSpec((2, 1, 1, BLOCK * group), lambda k: (0, k, 0, 0))
    prev_spec = pl.BlockSpec((2, 1, BLOCK, WIDTH), lambda k: (0, k, 0, 0))
    far_spec = pl.BlockSpec((3, 2, 1, BLOCK, WIDTH), lambda k: (0, 0, k, 0, 0))
    return pl.pallas_call(
        attend,
        grid=(key_heads,),
        in_specs=[
            pl.BlockSpec(memory_space=pltpu.SMEM),
            token_spec, token_spec, own_spec, got_spec, stat_spec, stat_spec,
        ],
        out_specs=[token_spec, own_spec, prev_spec, far_spec],
        out_shape=[
            jax.ShapeDtypeStruct(queries.shape, jnp.bfloat16),
            jax.ShapeDtypeStruct(own.shape, jnp.float32),
            jax.ShapeDtypeStruct((2, key_heads, BLOCK, WIDTH), jnp.float32),
            jax.ShapeDtypeStruct((3, 2, key_heads, BLOCK, WIDTH), jnp.float32),
        ],
        compiler_params=pltpu.CompilerParams(vmem_limit_bytes=VMEM_BYTES),
    )(kinds, queries, grads, own, got, logs, deltas)


def add_rows(index_ref, far_ref, hub_ref, out_ref):
    rows = far_ref[...]
    high = rows.astype(jnp.bfloat16)
    rest = rows - high.astype(jnp.float32)
    middle = rest.astype(jnp.bfloat16)
    low = (rest - middle.astype(jnp.float32)).astype(jnp.bfloat16)
    chunk = 256
    hub = jnp.sum(hub_ref[...], axis=0, keepdims=True)
    for start in range(0, out_ref.shape[0], chunk):
        block_at = lax.broadcasted_iota(jnp.int32, (chunk, rows.shape[0]), 0) + start
        chosen = jnp.where(block_at == index_ref[...], 1.0, 0.0).astype(jnp.bfloat16)
        total = sum(dot(chosen, part, ((1,), (0,))) for part in (high, middle, low))
        if start == 0:
            row_at = lax.broadcasted_iota(jnp.int32, total.shape, 0)
            total = total + jnp.where(row_at == 0, hub, 0.0)
        out_ref[start : start + chunk] = total


def scatter_rows(index, far, hub, blocks):
    return pl.pallas_call(
        add_rows,
        out_shape=jax.ShapeDtypeStruct((blocks, WIDTH), jnp.float32),
        compiler_params=pltpu.CompilerParams(vmem_limit_bytes=VMEM_BYTES),
    )(index, far, hub)


def shards(
    queries, key_states, value_states, out_grad, log_sums, row_deltas, block_pairs, pair_kinds
):
    devices = lax.axis_size("ctx") * lax.axis_size("head")
    tokens, key_heads, width = key_states.shape
    heads = queries.shape[1]
    group = heads // key_heads
    blocks = block_pairs.shape[0]
    rank = lax.axis_index("ctx") * lax.axis_size("head") + lax.axis_index("head")
    kinds = lax.dynamic_slice_in_dim(pair_kinds, rank * 2, 2, 0)

    stats = jnp.stack([log_sums, row_deltas])
    stats = lax.all_to_all(stats, "head", split_axis=2, concat_axis=1, tiled=True)
    stats = stats.reshape(2, key_heads, group, 2, BLOCK).transpose(0, 3, 1, 4, 2)
    stats = stats.reshape(2, 2, key_heads, 1, BLOCK * group)

    own = jnp.stack([key_states, value_states]).transpose(0, 2, 1, 3)
    pieces = own.reshape(2, key_heads, 2, BLOCK, width).transpose(0, 1, 3, 2, 4)
    pieces = pieces.reshape(devices, 2, width)
    rows = lax.all_to_all(pieces, AXES, split_axis=0, concat_axis=0, tiled=True)
    rows = rows.reshape(blocks, width)
    far = block_pairs[:, 3].reshape(devices, 2)
    before = jnp.maximum(2 * jnp.arange(devices, dtype=jnp.int32) - 1, 0)
    asked = jnp.stack([far[:, 0], far[:, 1], jnp.zeros_like(before), before], axis=1)
    chosen = (asked.reshape(-1)[:, None] == jnp.arange(blocks, dtype=jnp.int32)[None, :]).astype(
        jnp.bfloat16
    )
    picked = jnp.dot(chosen, rows, preferred_element_type=jnp.float32).astype(jnp.bfloat16)
    picked = picked.reshape(devices, 4, width)
    got = lax.all_to_all(picked, AXES, split_axis=0, concat_axis=0, tiled=True)
    got = got.transpose(1, 0, 2).reshape(4, 2, key_heads, BLOCK, width)

    dquery, down, dprev, dfar = attention(kinds, queries, out_grad, own, got, stats[0], stats[1])

    dprev = lax.ppermute(dprev, AXES, [(d, d - 1) for d in range(1, devices)])
    sent = dfar.reshape(3, devices, width).transpose(1, 0, 2)
    back = lax.all_to_all(sent, AXES, split_axis=0, concat_axis=0, tiled=True)
    sums = scatter_rows(
        block_pairs[:, 3].reshape(1, blocks), back[:, :2].reshape(blocks, width), back[:, 2], blocks
    )
    sums = sums.reshape(devices, 2, width)
    home = lax.all_to_all(sums, AXES, split_axis=0, concat_axis=0, tiled=True)
    home = home.reshape(2, key_heads, BLOCK, 2, width).transpose(0, 1, 3, 2, 4)
    total = down.reshape(home.shape) + home
    total = total.at[:, :, 1].add(dprev)
    total = total.reshape(2, key_heads, tokens, width).transpose(0, 2, 1, 3).astype(jnp.bfloat16)
    return dquery, total[0], total[1]


def solution(mesh):
    tokens = P(("ctx", "head"), None, None)
    stats = P("head", "ctx")
    return jax.shard_map(
        shards,
        mesh=mesh,
        in_specs=(tokens, tokens, tokens, tokens, stats, stats, P(), P()),
        out_specs=(tokens, tokens, tokens),
        check_vma=False,
    )
```

```python
import jax
import jax.numpy as jnp
from jax import lax
from jax.experimental import pallas as pl
from jax.experimental.pallas import tpu as pltpu
from jax.sharding import PartitionSpec as P

BLOCK = 64
WIDTH = 128
AXES = ("ctx", "head")
SPLIT = 4
PAIR = 2
SLOTS = SPLIT * PAIR + 2
HUB, BEFORE = SLOTS - 2, SLOTS - 1
VMEM_BYTES = 20 * 1024 * 1024
SLOW = pl.CostEstimate(flops=20_000_000_000, bytes_accessed=60_000_000, transcendentals=0)


def dot(left, right, contract=((1,), (0,))):
    return lax.dot_general(
        left, right, (contract, ((), ())), preferred_element_type=jnp.float32
    )


def strided(slot, kv):
    return pl.ds(kv * BLOCK * SLOTS + slot, BLOCK, stride=SLOTS)


def pack(head_ref, q_ref, g_ref, k_ref, v_ref, *rest):
    out_refs, pieces_ref, wide_ref = rest[:SPLIT], rest[SPLIT], rest[SPLIT + 1]
    tokens = q_ref.shape[0]
    half = wide_ref.shape[0] // 4
    for kv, ref in enumerate((k_ref, v_ref)):
        wide = ref[...].astype(jnp.float32).reshape(2 * half, WIDTH)
        for blk in range(PAIR):
            start = 2 * kv * half + blk
            wide_ref[pl.ds(start, half, stride=PAIR)] = wide[blk * half : (blk + 1) * half]
    pieces_ref[...] = wide_ref[...].astype(jnp.bfloat16)
    group = q_ref.shape[1] // SPLIT
    rows = tokens * group
    for k in range(SPLIT):
        for to in range(SPLIT):

            @pl.when(lax.rem(head_ref[0] + k, SPLIT) == to)
            def _(k=k, to=to):
                heads = slice(to * group, (to + 1) * group)
                out_refs[k][:rows] = q_ref[:, heads, :].reshape(rows, WIDTH)
                out_refs[k][rows : 2 * rows] = g_ref[:, heads, :].reshape(rows, WIDTH)
                out_refs[k][2 * rows : 2 * rows + tokens] = k_ref[:, to, :]
                out_refs[k][2 * rows + tokens :] = v_ref[:, to, :]


def packed(head, queries, grads, keys, values):
    tokens, heads, width = queries.shape
    part = jax.ShapeDtypeStruct((2 * tokens * (heads // SPLIT + 1), width), jnp.bfloat16)
    both = (2 * tokens * keys.shape[1], width)
    vmem = pl.BlockSpec(memory_space=pltpu.VMEM)
    return pl.pallas_call(
        pack,
        in_specs=[pl.BlockSpec(memory_space=pltpu.SMEM)] + [vmem] * 4,
        out_specs=[vmem] * (SPLIT + 1),
        out_shape=[part] * SPLIT + [jax.ShapeDtypeStruct(both, jnp.bfloat16)],
        scratch_shapes=[pltpu.VMEM(both, jnp.float32)],
        compiler_params=pltpu.CompilerParams(vmem_limit_bytes=VMEM_BYTES),
        cost_estimate=SLOW,
    )(head, queries, grads, keys, values)


def attend(head_ref, kinds, *refs):
    parts, (got_ref, log_ref, delta_ref), (dq_ref, own_ref, sent_ref) = refs[:4], refs[4:7], refs[7:10]
    wide_ref = refs[10]
    wide_ref[...] = got_ref[...].astype(jnp.float32)
    tokens = PAIR * BLOCK
    group = (parts[0].shape[0] - 2 * tokens) // (2 * tokens)
    rows = BLOCK * group
    scale = WIDTH ** (-0.5)
    key_at = lax.broadcasted_iota(jnp.int32, (BLOCK, rows), 0)
    token_at = lax.broadcasted_iota(jnp.int32, (BLOCK, rows), 1) // group
    causal = key_at <= token_at
    table_at = 2 * tokens * group

    def own(sender, kv, blk):
        start = table_at + kv * tokens + blk * BLOCK
        return parts[sender][start : start + BLOCK]

    def got(slot, kv):
        return wide_ref[strided(slot, kv)].astype(jnp.bfloat16)

    owner = [lax.rem(head_ref[0] + SPLIT - k, SPLIT) for k in range(SPLIT)]
    terms = {}
    for k in range(SPLIT):
        for blk in range(PAIR):
            at = owner[k] * PAIR + blk
            tables = []
            for kv in range(2):
                if blk:
                    before = own(k, kv, 0)
                else:
                    before = jnp.where(owner[k] == 0, got(BEFORE, kv), own((k + 1) % SPLIT, kv, 1))
                tables.append(
                    jnp.concatenate([own(k, kv, blk), before, got(HUB, kv), got(at, kv)], axis=0)
                )
            keys, values = tables
            queries = parts[k][blk * rows : (blk + 1) * rows]
            grads = parts[k][tokens * group + blk * rows : tokens * group + (blk + 1) * rows]
            scores = dot(keys, queries, ((1,), (1,))) * scale
            weights = jnp.exp(scores - log_ref[at])
            masked = [jnp.where(causal, weights[:BLOCK], 0.0)]
            for slot in range(1, 4):
                live = kinds[at, slot] > 0
                masked.append(jnp.where(live, weights[slot * BLOCK : (slot + 1) * BLOCK], 0.0))
            weights = jnp.concatenate(masked, axis=0)
            prob_grad = dot(values, grads, ((1,), (1,)))
            dscore = (weights * (prob_grad - delta_ref[at])).astype(jnp.bfloat16)
            dvalue = dot(weights.astype(jnp.bfloat16), grads)
            dkey = dot(dscore, queries) * scale
            dquery = dot(dscore, keys, ((0,), (0,))) * scale
            dq_ref[k, blk * rows : (blk + 1) * rows] = dquery.astype(jnp.bfloat16)
            terms[k, blk] = (dkey, dvalue)
    for kv in range(2):

        def piece(k, blk, slot):
            return terms[k, blk][kv][slot * BLOCK : (slot + 1) * BLOCK]

        hub = 0.0
        outside = 0.0
        for k in range(SPLIT):
            for blk in range(PAIR):
                sent_ref[strided(owner[k] * PAIR + blk, kv)] = piece(k, blk, 3)
                hub = hub + piece(k, blk, 2)
            outside = outside + jnp.where(owner[k] == 0, piece(k, 0, 1), 0.0)
            later = (k + SPLIT - 1) % SPLIT
            own_ref[k, kv, :BLOCK] = piece(k, 0, 0) + piece(k, 1, 1)
            own_ref[k, kv, BLOCK:] = piece(k, 1, 0) + jnp.where(
                owner[later] == 0, 0.0, piece(later, 0, 1)
            )
        sent_ref[strided(HUB, kv)] = hub
        sent_ref[strided(BEFORE, kv)] = outside


def attention(head, kinds, parts, got, logs, deltas):
    tokens = PAIR * BLOCK
    group = (parts[0].shape[0] - 2 * tokens) // (2 * tokens)
    vmem = pl.BlockSpec(memory_space=pltpu.VMEM)
    smem = pl.BlockSpec(memory_space=pltpu.SMEM)
    return pl.pallas_call(
        attend,
        in_specs=[smem, smem] + [vmem] * (SPLIT + 3),
        out_specs=[vmem] * 3,
        out_shape=[
            jax.ShapeDtypeStruct((SPLIT, tokens * group, WIDTH), jnp.bfloat16),
            jax.ShapeDtypeStruct((SPLIT, 2, tokens, WIDTH), jnp.float32),
            jax.ShapeDtypeStruct(got.shape, jnp.float32),
        ],
        scratch_shapes=[pltpu.VMEM(got.shape, jnp.float32)],
        compiler_params=pltpu.CompilerParams(vmem_limit_bytes=VMEM_BYTES),
        cost_estimate=pl.CostEstimate(
            flops=1_400_000_000, bytes_accessed=8_000_000, transcendentals=1_000_000
        ),
    )(head, kinds, *parts, got, logs, deltas)


def pack_back(dq_ref, own_ref, *out_refs):
    rows, tokens = dq_ref.shape[1], own_ref.shape[2]
    for k in range(SPLIT):
        out_refs[k][:rows] = dq_ref[k]
        for kv in range(2):
            total = own_ref[k, kv]
            high = total.astype(jnp.bfloat16)
            low = (total - high.astype(jnp.float32)).astype(jnp.bfloat16)
            start = rows + kv * tokens
            out_refs[k][start : start + tokens] = high
            start = start + 2 * tokens
            out_refs[k][start : start + tokens] = low


def packed_back(dquery, own):
    part = jax.ShapeDtypeStruct((dquery.shape[1] + 4 * own.shape[2], WIDTH), jnp.bfloat16)
    vmem = pl.BlockSpec(memory_space=pltpu.VMEM)
    return pl.pallas_call(
        pack_back,
        in_specs=[vmem] * 2,
        out_specs=[vmem] * SPLIT,
        out_shape=[part] * SPLIT,
        compiler_params=pltpu.CompilerParams(vmem_limit_bytes=VMEM_BYTES),
        cost_estimate=SLOW,
    )(dquery, own)


def unpack(head_ref, *refs):
    parts, (dq_ref, own_ref) = refs[:SPLIT], refs[SPLIT:]
    tokens = dq_ref.shape[0]
    group = dq_ref.shape[1] // SPLIT
    rows = tokens * group
    for k in range(SPLIT):
        for source in range(SPLIT):

            @pl.when(lax.rem(head_ref[0] + k, SPLIT) == source)
            def _(k=k, source=source):
                heads = slice(source * group, (source + 1) * group)
                dq_ref[:, heads, :] = parts[k][:rows].reshape(tokens, group, WIDTH)
                for kv in range(2):
                    start = rows + kv * tokens
                    high = parts[k][start : start + tokens].astype(jnp.float32)
                    start = start + 2 * tokens
                    low = parts[k][start : start + tokens].astype(jnp.float32)
                    own_ref[kv, :, source, :] = high + low


def unpacked(head, parts, queries, keys):
    vmem = pl.BlockSpec(memory_space=pltpu.VMEM)
    return pl.pallas_call(
        unpack,
        in_specs=[pl.BlockSpec(memory_space=pltpu.SMEM)] + [vmem] * SPLIT,
        out_specs=[vmem] * 2,
        out_shape=[
            jax.ShapeDtypeStruct(queries.shape, jnp.bfloat16),
            jax.ShapeDtypeStruct((2,) + keys.shape, jnp.float32),
        ],
        compiler_params=pltpu.CompilerParams(vmem_limit_bytes=VMEM_BYTES),
        cost_estimate=SLOW,
    )(head, *parts)


def finish(home_ref, own_ref, *out_refs):
    rows = own_ref.shape[0] // 2
    half = rows // PAIR
    for kv in range(2):
        for blk in range(PAIR):
            start = blk * half
            total = home_ref[pl.ds(kv * rows + blk, half, stride=PAIR)]
            total = total + own_ref[kv * rows + start : kv * rows + start + half]
            out_refs[kv][start : start + half] = total.astype(jnp.bfloat16)


def finished(home, own):
    out = jax.ShapeDtypeStruct((own.shape[0] // 2, WIDTH), jnp.bfloat16)
    return pl.pallas_call(
        finish,
        out_shape=[out] * 2,
        compiler_params=pltpu.CompilerParams(vmem_limit_bytes=VMEM_BYTES),
    )(home, own)


def pick_rows(index_ref, rows_ref, out_ref):
    blocks = rows_ref.shape[0]
    chunk = 256
    block_at = lax.broadcasted_iota(jnp.int32, (chunk, blocks), 1)
    rows = rows_ref[...]
    for start in range(0, out_ref.shape[0], chunk):
        here = slice(start, start + chunk)
        chosen = jnp.where(block_at == index_ref[here], 1.0, 0.0).astype(jnp.bfloat16)
        out_ref[here] = dot(chosen, rows).astype(jnp.bfloat16)


def gather_rows(index, rows):
    return pl.pallas_call(
        pick_rows,
        out_shape=jax.ShapeDtypeStruct((index.shape[0], WIDTH), jnp.bfloat16),
        compiler_params=pltpu.CompilerParams(vmem_limit_bytes=VMEM_BYTES),
    )(index, rows)


def add_rows(index_ref, rows_ref, out_ref):
    rows = rows_ref[...]
    high = rows.astype(jnp.bfloat16)
    rest = rows - high.astype(jnp.float32)
    middle = rest.astype(jnp.bfloat16)
    low = (rest - middle.astype(jnp.float32)).astype(jnp.bfloat16)
    chunk = 256
    for start in range(0, out_ref.shape[0], chunk):
        block_at = lax.broadcasted_iota(jnp.int32, (chunk, rows.shape[0]), 0) + start
        chosen = jnp.where(block_at == index_ref[...], 1.0, 0.0).astype(jnp.bfloat16)
        out_ref[start : start + chunk] = dot(chosen, high) + dot(chosen, middle) + dot(chosen, low)


def scatter_rows(index, rows, blocks):
    return pl.pallas_call(
        add_rows,
        out_shape=jax.ShapeDtypeStruct((blocks, WIDTH), jnp.float32),
        compiler_params=pltpu.CompilerParams(vmem_limit_bytes=VMEM_BYTES),
    )(index, rows)


def shards(
    queries, key_states, value_states, out_grad, log_sums, row_deltas, block_pairs, pair_kinds
):
    shard_count = lax.axis_size("ctx")
    devices = shard_count * SPLIT
    tokens, key_heads, width = key_states.shape
    heads = queries.shape[1]
    group = heads // key_heads
    blocks = block_pairs.shape[0]
    here = SPLIT * PAIR
    rank, head = lax.axis_index("ctx"), lax.axis_index("head")
    head_at = head.reshape(1)
    wire = (shard_count, SLOTS // 2, 2, width)

    def exchange(array, axes):
        return lax.all_to_all(array, axes, split_axis=0, concat_axis=0, tiled=True)

    *parts, pieces = packed(head_at, queries, out_grad, key_states, value_states)
    rows = exchange(pieces.reshape(devices, PAIR, width), AXES).reshape(blocks, width)

    far = block_pairs[:, 3].reshape(shard_count, here)
    before = jnp.maximum(here * jnp.arange(shard_count, dtype=jnp.int32) - 1, 0)
    index = jnp.concatenate([far, jnp.zeros_like(before)[:, None], before[:, None]], axis=1)
    kinds = lax.dynamic_slice_in_dim(pair_kinds, rank * here, here, 0)
    stats = jnp.stack([log_sums, row_deltas]).transpose(0, 2, 1)
    stats = stats.reshape(2, here, 1, BLOCK * group)
    index, kinds, logs, deltas = lax.optimization_barrier((index, kinds, stats[0], stats[1]))
    got = exchange(gather_rows(index.reshape(-1, 1), rows).reshape(wire), "ctx")

    for k in (2, 1, 3):
        if k == 1:
            parts = list(lax.optimization_barrier(parts))
        parts[k] = lax.ppermute(parts[k], "head", [(i, (i + k) % SPLIT) for i in range(SPLIT)])
    dquery, own, sent = attention(head_at, kinds, parts, got.reshape(-1, width), logs, deltas)

    back = exchange(sent.reshape(wire), "ctx")
    sums = scatter_rows(index.reshape(1, -1), back.reshape(-1, width), blocks)
    home = exchange(sums.reshape(devices, PAIR, width), AXES)

    parts = list(packed_back(dquery, own))
    for k in range(1, SPLIT):
        parts[k] = lax.ppermute(parts[k], "head", [(i, (i - k) % SPLIT) for i in range(SPLIT)])
    dquery, own = unpacked(head_at, parts, queries, key_states)

    dkey, dvalue = finished(home.reshape(-1, width), own.reshape(-1, width))
    return dquery, dkey.reshape(key_states.shape), dvalue.reshape(key_states.shape)


def solution(mesh):
    tokens = P(("ctx", "head"), None, None)
    stats = P("head", "ctx")
    return jax.shard_map(
        shards,
        mesh=mesh,
        in_specs=(tokens, tokens, tokens, tokens, stats, stats, P(), P()),
        out_specs=(tokens, tokens, tokens),
        check_vma=False,
    )
```

```python
import functools

import jax
import jax.numpy as jnp
from jax import lax
from jax.experimental import pallas as pl
from jax.experimental.pallas import tpu as pltpu
from jax.sharding import PartitionSpec as P

BLOCK = 64
WIDTH = 128
AXES = ("ctx", "head")
SPLIT = 4
PAIR = 2
SLOTS = SPLIT * PAIR + 2
HUB, BEFORE = SLOTS - 2, SLOTS - 1
VMEM_BYTES = 20 * 1024 * 1024
SLOW = pl.CostEstimate(flops=20_000_000_000, bytes_accessed=60_000_000, transcendentals=0)


def dot(left, right, contract=((1,), (0,))):
    return lax.dot_general(
        left, right, (contract, ((), ())), preferred_element_type=jnp.float32
    )


def strided(slot, kv):
    return pl.ds(kv * BLOCK * SLOTS + slot, BLOCK, stride=SLOTS)


def interleave(k_ref, v_ref, pieces_ref, wide_ref):
    half = wide_ref.shape[0] // 4
    for kv, ref in enumerate((k_ref, v_ref)):
        wide = ref[...].astype(jnp.float32)
        for blk in range(PAIR):
            start = 2 * kv * half + blk
            wide_ref[pl.ds(start, half, stride=PAIR)] = wide[blk * half : (blk + 1) * half]
    pieces_ref[...] = wide_ref[...].astype(jnp.bfloat16)


def interleaved(keys, values):
    both = (2 * keys.shape[0], WIDTH)
    return pl.pallas_call(
        interleave,
        out_shape=jax.ShapeDtypeStruct(both, jnp.bfloat16),
        scratch_shapes=[pltpu.VMEM(both, jnp.float32)],
        compiler_params=pltpu.CompilerParams(vmem_limit_bytes=VMEM_BYTES),
    )(keys, values)


def pack(steps, head_ref, q_ref, g_ref, k_ref, v_ref, *out_refs):
    tokens = q_ref.shape[0]
    group = q_ref.shape[1] // SPLIT
    rows = tokens * group
    for out_ref, k in zip(out_refs, steps):
        for to in range(SPLIT):

            @pl.when(lax.rem(head_ref[0] + k, SPLIT) == to)
            def _(out_ref=out_ref, to=to):
                heads = slice(to * group, (to + 1) * group)
                out_ref[:rows] = q_ref[:, heads, :].reshape(rows, WIDTH)
                out_ref[rows : 2 * rows] = g_ref[:, heads, :].reshape(rows, WIDTH)
                out_ref[2 * rows : 2 * rows + tokens] = k_ref[:, to, :]
                out_ref[2 * rows + tokens :] = v_ref[:, to, :]


def packed(steps, head, queries, grads, keys, values):
    tokens, heads, width = queries.shape
    part = jax.ShapeDtypeStruct((2 * tokens * (heads // SPLIT + 1), width), jnp.bfloat16)
    return pl.pallas_call(
        functools.partial(pack, steps),
        in_specs=[pl.BlockSpec(memory_space=pltpu.SMEM)] + [pl.BlockSpec()] * 4,
        out_specs=[pl.BlockSpec()] * len(steps),
        out_shape=[part] * len(steps),
        compiler_params=pltpu.CompilerParams(vmem_limit_bytes=VMEM_BYTES),
        cost_estimate=SLOW,
    )(head, queries, grads, keys, values)


def attend(head_ref, kinds, *refs):
    parts, (got_ref, log_ref, delta_ref), (dq_ref, own_ref, sent_ref) = refs[:4], refs[4:7], refs[7:10]
    wide_ref = refs[10]
    wide_ref[...] = got_ref[...].astype(jnp.float32)
    tokens = PAIR * BLOCK
    group = (parts[0].shape[0] - 2 * tokens) // (2 * tokens)
    rows = BLOCK * group
    scale = WIDTH ** (-0.5)
    key_at = lax.broadcasted_iota(jnp.int32, (BLOCK, rows), 0)
    token_at = lax.broadcasted_iota(jnp.int32, (BLOCK, rows), 1) // group
    causal = key_at <= token_at
    table_at = 2 * tokens * group

    def own(sender, kv, blk):
        start = table_at + kv * tokens + blk * BLOCK
        return parts[sender][start : start + BLOCK]

    def got(slot, kv):
        return wide_ref[strided(slot, kv)].astype(jnp.bfloat16)

    owner = [lax.rem(head_ref[0] + SPLIT - k, SPLIT) for k in range(SPLIT)]
    terms = {}
    for k in range(SPLIT):
        for blk in range(PAIR):
            at = owner[k] * PAIR + blk
            tables = []
            for kv in range(2):
                if blk:
                    before = own(k, kv, 0)
                else:
                    before = jnp.where(owner[k] == 0, got(BEFORE, kv), own((k + 1) % SPLIT, kv, 1))
                tables.append(
                    jnp.concatenate([own(k, kv, blk), before, got(HUB, kv), got(at, kv)], axis=0)
                )
            keys, values = tables
            queries = parts[k][blk * rows : (blk + 1) * rows]
            grads = parts[k][tokens * group + blk * rows : tokens * group + (blk + 1) * rows]
            scores = dot(keys, queries, ((1,), (1,))) * scale
            weights = jnp.exp(scores - log_ref[at])
            masked = [jnp.where(causal, weights[:BLOCK], 0.0)]
            for slot in range(1, 4):
                live = kinds[at, slot] > 0
                masked.append(jnp.where(live, weights[slot * BLOCK : (slot + 1) * BLOCK], 0.0))
            weights = jnp.concatenate(masked, axis=0)
            prob_grad = dot(values, grads, ((1,), (1,)))
            dscore = (weights * (prob_grad - delta_ref[at])).astype(jnp.bfloat16)
            dvalue = dot(weights.astype(jnp.bfloat16), grads)
            dkey = dot(dscore, queries) * scale
            dquery = dot(dscore, keys, ((0,), (0,))) * scale
            dq_ref[k, blk * rows : (blk + 1) * rows] = dquery.astype(jnp.bfloat16)
            terms[k, blk] = (dkey, dvalue)
    for kv in range(2):

        def piece(k, blk, slot):
            return terms[k, blk][kv][slot * BLOCK : (slot + 1) * BLOCK]

        hub = 0.0
        outside = 0.0
        for k in range(SPLIT):
            for blk in range(PAIR):
                sent_ref[strided(owner[k] * PAIR + blk, kv)] = piece(k, blk, 3)
                hub = hub + piece(k, blk, 2)
            outside = outside + jnp.where(owner[k] == 0, piece(k, 0, 1), 0.0)
            later = (k + SPLIT - 1) % SPLIT
            own_ref[k, kv, :BLOCK] = piece(k, 0, 0) + piece(k, 1, 1)
            own_ref[k, kv, BLOCK:] = piece(k, 1, 0) + jnp.where(
                owner[later] == 0, 0.0, piece(later, 0, 1)
            )
        sent_ref[strided(HUB, kv)] = hub
        sent_ref[strided(BEFORE, kv)] = outside


def attention(head, kinds, parts, got, logs, deltas):
    tokens = PAIR * BLOCK
    group = (parts[0].shape[0] - 2 * tokens) // (2 * tokens)
    vmem = pl.BlockSpec(memory_space=pltpu.VMEM)
    smem = pl.BlockSpec(memory_space=pltpu.SMEM)
    return pl.pallas_call(
        attend,
        in_specs=[smem, smem] + [vmem] * (SPLIT + 3),
        out_specs=[vmem] * 3,
        out_shape=[
            jax.ShapeDtypeStruct((SPLIT, tokens * group, WIDTH), jnp.bfloat16),
            jax.ShapeDtypeStruct((SPLIT, 2, tokens, WIDTH), jnp.float32),
            jax.ShapeDtypeStruct(got.shape, jnp.float32),
        ],
        scratch_shapes=[pltpu.VMEM(got.shape, jnp.float32)],
        compiler_params=pltpu.CompilerParams(vmem_limit_bytes=VMEM_BYTES),
        cost_estimate=pl.CostEstimate(
            flops=1_400_000_000, bytes_accessed=8_000_000, transcendentals=1_000_000
        ),
    )(head, kinds, *parts, got, logs, deltas)


def pack_back(dq_ref, own_ref, *out_refs):
    rows, tokens = dq_ref.shape[1], own_ref.shape[2]
    for k in range(SPLIT):
        out_refs[k][:rows] = dq_ref[k]
        for kv in range(2):
            total = own_ref[k, kv]
            high = total.astype(jnp.bfloat16)
            low = (total - high.astype(jnp.float32)).astype(jnp.bfloat16)
            start = rows + kv * tokens
            out_refs[k][start : start + tokens] = high
            start = start + 2 * tokens
            out_refs[k][start : start + tokens] = low


def packed_back(dquery, own):
    part = jax.ShapeDtypeStruct((dquery.shape[1] + 4 * own.shape[2], WIDTH), jnp.bfloat16)
    vmem = pl.BlockSpec(memory_space=pltpu.VMEM)
    return pl.pallas_call(
        pack_back,
        in_specs=[vmem] * 2,
        out_specs=[vmem] * SPLIT,
        out_shape=[part] * SPLIT,
        compiler_params=pltpu.CompilerParams(vmem_limit_bytes=VMEM_BYTES),
        cost_estimate=SLOW,
    )(dquery, own)


def unpack(head_ref, *refs):
    parts, (dq_ref, own_ref) = refs[:SPLIT], refs[SPLIT:]
    tokens = dq_ref.shape[0]
    group = dq_ref.shape[1] // SPLIT
    rows = tokens * group
    for k in range(SPLIT):
        for source in range(SPLIT):

            @pl.when(lax.rem(head_ref[0] + k, SPLIT) == source)
            def _(k=k, source=source):
                heads = slice(source * group, (source + 1) * group)
                dq_ref[:, heads, :] = parts[k][:rows].reshape(tokens, group, WIDTH)
                for kv in range(2):
                    start = rows + kv * tokens
                    high = parts[k][start : start + tokens].astype(jnp.float32)
                    start = start + 2 * tokens
                    low = parts[k][start : start + tokens].astype(jnp.float32)
                    own_ref[kv, :, source, :] = high + low


def unpacked(head, parts, queries, keys):
    vmem = pl.BlockSpec(memory_space=pltpu.VMEM)
    return pl.pallas_call(
        unpack,
        in_specs=[pl.BlockSpec(memory_space=pltpu.SMEM)] + [vmem] * SPLIT,
        out_specs=[vmem] * 2,
        out_shape=[
            jax.ShapeDtypeStruct(queries.shape, jnp.bfloat16),
            jax.ShapeDtypeStruct((2,) + keys.shape, jnp.float32),
        ],
        compiler_params=pltpu.CompilerParams(vmem_limit_bytes=VMEM_BYTES),
        cost_estimate=SLOW,
    )(head, *parts)


def finish(home_ref, own_ref, *out_refs):
    rows = own_ref.shape[0] // 2
    half = rows // PAIR
    for kv in range(2):
        for blk in range(PAIR):
            start = blk * half
            total = home_ref[pl.ds(kv * rows + blk, half, stride=PAIR)]
            total = total + own_ref[kv * rows + start : kv * rows + start + half]
            out_refs[kv][start : start + half] = total.astype(jnp.bfloat16)


def finished(home, own):
    out = jax.ShapeDtypeStruct((own.shape[0] // 2, WIDTH), jnp.bfloat16)
    return pl.pallas_call(
        finish,
        out_shape=[out] * 2,
        compiler_params=pltpu.CompilerParams(vmem_limit_bytes=VMEM_BYTES),
    )(home, own)


def pick_rows(index_ref, rows_ref, out_ref):
    blocks = rows_ref.shape[0]
    chunk = 256
    block_at = lax.broadcasted_iota(jnp.int32, (chunk, blocks), 1)
    rows = rows_ref[...]
    for start in range(0, out_ref.shape[0], chunk):
        here = slice(start, start + chunk)
        chosen = jnp.where(block_at == index_ref[here], 1.0, 0.0).astype(jnp.bfloat16)
        out_ref[here] = dot(chosen, rows).astype(jnp.bfloat16)


def gather_rows(index, rows):
    return pl.pallas_call(
        pick_rows,
        out_shape=jax.ShapeDtypeStruct((index.shape[0], WIDTH), jnp.bfloat16),
        compiler_params=pltpu.CompilerParams(vmem_limit_bytes=VMEM_BYTES),
        cost_estimate=pl.CostEstimate(flops=5_000_000_000, bytes_accessed=15_000_000, transcendentals=0),
    )(index, rows)


def add_rows(index_ref, rows_ref, out_ref):
    rows = rows_ref[...]
    high = rows.astype(jnp.bfloat16)
    rest = rows - high.astype(jnp.float32)
    middle = rest.astype(jnp.bfloat16)
    low = (rest - middle.astype(jnp.float32)).astype(jnp.bfloat16)
    chunk = 256
    for start in range(0, out_ref.shape[0], chunk):
        block_at = lax.broadcasted_iota(jnp.int32, (chunk, rows.shape[0]), 0) + start
        chosen = jnp.where(block_at == index_ref[...], 1.0, 0.0).astype(jnp.bfloat16)
        out_ref[start : start + chunk] = dot(chosen, high) + dot(chosen, middle) + dot(chosen, low)


def scatter_rows(index, rows, blocks):
    return pl.pallas_call(
        add_rows,
        out_shape=jax.ShapeDtypeStruct((blocks, WIDTH), jnp.float32),
        compiler_params=pltpu.CompilerParams(vmem_limit_bytes=VMEM_BYTES),
    )(index, rows)


def shards(
    queries, key_states, value_states, out_grad, log_sums, row_deltas, block_pairs, pair_kinds
):
    shard_count = lax.axis_size("ctx")
    devices = shard_count * SPLIT
    tokens, key_heads, width = key_states.shape
    heads = queries.shape[1]
    group = heads // key_heads
    blocks = block_pairs.shape[0]
    here = SPLIT * PAIR
    rank, head = lax.axis_index("ctx"), lax.axis_index("head")
    head_at = head.reshape(1)
    wire = (shard_count, SLOTS // 2, 2, width)

    def exchange(array, axes):
        return lax.all_to_all(array, axes, split_axis=0, concat_axis=0, tiled=True)

    pieces = interleaved(key_states.reshape(-1, width), value_states.reshape(-1, width))
    rows = exchange(pieces.reshape(devices, PAIR, width), AXES).reshape(blocks, width)

    far = block_pairs[:, 3].reshape(shard_count, here)
    before = jnp.maximum(here * jnp.arange(shard_count, dtype=jnp.int32) - 1, 0)
    index = jnp.concatenate([far, jnp.zeros_like(before)[:, None], before[:, None]], axis=1)
    kinds = lax.dynamic_slice_in_dim(pair_kinds, rank * here, here, 0)
    stats = jnp.stack([log_sums, row_deltas]).transpose(0, 2, 1)
    stats = stats.reshape(2, here, 1, BLOCK * group)
    later = lax.optimization_barrier((pieces, queries, out_grad, key_states, value_states))
    parts = packed((1, 2, 3), head_at, *later[1:])
    index, kinds, logs, deltas, *parts = lax.optimization_barrier(
        (index, kinds, stats[0], stats[1], *parts)
    )
    got = exchange(gather_rows(index.reshape(-1, 1), rows).reshape(wire), "ctx")

    ready = lax.optimization_barrier((rows, queries, out_grad, key_states, value_states))
    parts = [*packed((0,), head_at, *ready[1:]), *parts]
    for k in (2, 1, 3):
        if k == 1:
            parts[1:] = lax.optimization_barrier(parts[1:])
        parts[k] = lax.ppermute(parts[k], "head", [(i, (i + k) % SPLIT) for i in range(SPLIT)])
    dquery, own, sent = attention(head_at, kinds, parts, got.reshape(-1, width), logs, deltas)

    back = exchange(sent.reshape(shard_count, 1, SLOTS * width), "ctx")
    sums = scatter_rows(index.reshape(1, -1), back.reshape(-1, width), blocks)
    home = exchange(sums.reshape(devices, PAIR, width), AXES)

    parts = list(packed_back(dquery, own))
    for k in range(1, SPLIT):
        parts[k] = lax.ppermute(parts[k], "head", [(i, (i - k) % SPLIT) for i in range(SPLIT)])
    dquery, own = unpacked(head_at, parts, queries, key_states)

    dkey, dvalue = finished(home.reshape(-1, width), own.reshape(-1, width))
    return dquery, dkey.reshape(key_states.shape), dvalue.reshape(key_states.shape)


def solution(mesh):
    tokens = P(("ctx", "head"), None, None)
    stats = P("head", "ctx")
    return jax.shard_map(
        shards,
        mesh=mesh,
        in_specs=(tokens, tokens, tokens, tokens, stats, stats, P(), P()),
        out_specs=(tokens, tokens, tokens),
        check_vma=False,
    )
```

```python
import jax
import jax.numpy as jnp
from jax import lax
from jax.experimental import pallas as pl
from jax.experimental.pallas import tpu as pltpu
from jax.sharding import PartitionSpec as P

BLOCK = 64
WIDTH = 128
AXES = ("ctx", "head")
SPLIT = 4
PAIR = 2
SLOTS = SPLIT * PAIR + 2
HUB, BEFORE = SLOTS - 2, SLOTS - 1
VMEM_BYTES = 20 * 1024 * 1024
WHOLE_VMEM = 60 * 1024 * 1024
SLOW = pl.CostEstimate(flops=20_000_000_000, bytes_accessed=60_000_000, transcendentals=0)


def dot(left, right, contract=((1,), (0,))):
    return lax.dot_general(
        left, right, (contract, ((), ())), preferred_element_type=jnp.float32
    )


def three_parts(rows):
    high = rows.astype(jnp.bfloat16)
    rest = rows - high.astype(jnp.float32)
    middle = rest.astype(jnp.bfloat16)
    return high, middle, (rest - middle.astype(jnp.float32)).astype(jnp.bfloat16)


def strided(slot, kv):
    return pl.ds(kv * BLOCK * SLOTS + slot, BLOCK, stride=SLOTS)


def interleave(k_ref, v_ref, pieces_ref, wide_ref):
    half = wide_ref.shape[0] // 4
    for kv, ref in enumerate((k_ref, v_ref)):
        wide = ref[...].astype(jnp.float32)
        for blk in range(PAIR):
            start = 2 * kv * half + blk
            wide_ref[pl.ds(start, half, stride=PAIR)] = wide[blk * half : (blk + 1) * half]
    pieces_ref[...] = wide_ref[...].astype(jnp.bfloat16)


def interleaved(keys, values):
    both = (2 * keys.shape[0], WIDTH)
    return pl.pallas_call(
        interleave,
        out_shape=jax.ShapeDtypeStruct(both, jnp.bfloat16),
        scratch_shapes=[pltpu.VMEM(both, jnp.float32)],
        compiler_params=pltpu.CompilerParams(vmem_limit_bytes=WHOLE_VMEM),
    )(keys, values)


def pack(head_ref, q_ref, g_ref, k_ref, v_ref, *out_refs):
    tokens = q_ref.shape[0]
    group = q_ref.shape[1] // SPLIT
    rows = tokens * group
    for k in range(SPLIT):
        for to in range(SPLIT):

            @pl.when(lax.rem(head_ref[0] + k, SPLIT) == to)
            def _(k=k, to=to):
                heads = slice(to * group, (to + 1) * group)
                out_refs[k][:rows] = q_ref[:, heads, :].reshape(rows, WIDTH)
                out_refs[k][rows : 2 * rows] = g_ref[:, heads, :].reshape(rows, WIDTH)
                out_refs[k][2 * rows : 2 * rows + tokens] = k_ref[:, to, :]
                out_refs[k][2 * rows + tokens :] = v_ref[:, to, :]


def packed(head, queries, grads, keys, values):
    tokens, heads, width = queries.shape
    part = jax.ShapeDtypeStruct((2 * tokens * (heads // SPLIT + 1), width), jnp.bfloat16)
    return pl.pallas_call(
        pack,
        in_specs=[pl.BlockSpec(memory_space=pltpu.SMEM)] + [pl.BlockSpec()] * 4,
        out_specs=[pl.BlockSpec()] * SPLIT,
        out_shape=[part] * SPLIT,
        compiler_params=pltpu.CompilerParams(vmem_limit_bytes=WHOLE_VMEM),
        cost_estimate=SLOW,
    )(head, queries, grads, keys, values)


def spread(*refs):
    stat_refs, row_refs = refs[:2], refs[2:]
    group = stat_refs[0].shape[0]
    columns = BLOCK * group
    stats = jnp.concatenate([ref[...] for ref in stat_refs], axis=0)
    stats = jnp.concatenate(three_parts(stats), axis=0)
    token_at = lax.broadcasted_iota(jnp.int32, (BLOCK, columns), 0)
    column_at = lax.broadcasted_iota(jnp.int32, (BLOCK, columns), 1)
    copies = jnp.where(token_at == column_at // group, 1.0, 0.0).astype(jnp.bfloat16)
    head_at = lax.broadcasted_iota(jnp.int32, (group, columns), 0)
    mine = head_at == lax.broadcasted_iota(jnp.int32, (group, columns), 1) % group
    for at in range(SPLIT * PAIR):
        wide = dot(stats[:, at * BLOCK : (at + 1) * BLOCK], copies)
        for which, row_ref in enumerate(row_refs):
            starts = [(2 * part + which) * group for part in range(3)]
            value = sum(wide[start : start + group] for start in starts)
            row_ref[at] = jnp.sum(jnp.where(mine, value, 0.0), axis=0, keepdims=True)


def spread_rows(*stats):
    vmem = pl.BlockSpec(memory_space=pltpu.VMEM)
    row = jax.ShapeDtypeStruct((SPLIT * PAIR, 1, BLOCK * stats[0].shape[0]), jnp.float32)
    return pl.pallas_call(
        spread,
        in_specs=[vmem] * 2,
        out_specs=[vmem] * 2,
        out_shape=[row, row],
        compiler_params=pltpu.CompilerParams(vmem_limit_bytes=VMEM_BYTES),
        cost_estimate=SLOW,
    )(*stats)


def attend(head_ref, kinds, *refs):
    parts, (got_ref, log_ref, delta_ref), (dq_ref, own_ref, sent_ref) = refs[:4], refs[4:7], refs[7:10]
    wide_ref = refs[10]
    wide_ref[...] = got_ref[...].astype(jnp.float32)
    tokens = PAIR * BLOCK
    group = (parts[0].shape[0] - 2 * tokens) // (2 * tokens)
    rows = BLOCK * group
    scale = WIDTH ** (-0.5)
    key_at = lax.broadcasted_iota(jnp.int32, (BLOCK, rows), 0)
    token_at = lax.broadcasted_iota(jnp.int32, (BLOCK, rows), 1) // group
    causal = key_at <= token_at
    table_at = 2 * tokens * group

    def own(sender, kv, blk):
        start = table_at + kv * tokens + blk * BLOCK
        return parts[sender][start : start + BLOCK]

    def got(slot, kv):
        return wide_ref[strided(slot, kv)].astype(jnp.bfloat16)

    owner = [lax.rem(head_ref[0] + SPLIT - k, SPLIT) for k in range(SPLIT)]
    terms = {}
    for k in range(SPLIT):
        for blk in range(PAIR):
            at = owner[k] * PAIR + blk
            tables = []
            for kv in range(2):
                if blk:
                    before = own(k, kv, 0)
                else:
                    before = jnp.where(owner[k] == 0, got(BEFORE, kv), own((k + 1) % SPLIT, kv, 1))
                tables.append(
                    jnp.concatenate([own(k, kv, blk), before, got(HUB, kv), got(at, kv)], axis=0)
                )
            keys, values = tables
            queries = parts[k][blk * rows : (blk + 1) * rows]
            grads = parts[k][tokens * group + blk * rows : tokens * group + (blk + 1) * rows]
            scores = dot(keys, queries, ((1,), (1,))) * scale
            weights = jnp.exp(scores - log_ref[at])
            masked = [jnp.where(causal, weights[:BLOCK], 0.0)]
            for slot in range(1, 4):
                live = kinds[at, slot] > 0
                masked.append(jnp.where(live, weights[slot * BLOCK : (slot + 1) * BLOCK], 0.0))
            weights = jnp.concatenate(masked, axis=0)
            prob_grad = dot(values, grads, ((1,), (1,)))
            dscore = (weights * (prob_grad - delta_ref[at])).astype(jnp.bfloat16)
            dvalue = dot(weights.astype(jnp.bfloat16), grads)
            dkey = dot(dscore, queries) * scale
            dquery = dot(dscore, keys, ((0,), (0,))) * scale
            dq_ref[k, blk * rows : (blk + 1) * rows] = dquery.astype(jnp.bfloat16)
            terms[k, blk] = (dkey, dvalue)
    for kv in range(2):

        def piece(k, blk, slot):
            return terms[k, blk][kv][slot * BLOCK : (slot + 1) * BLOCK]

        hub = 0.0
        outside = 0.0
        for k in range(SPLIT):
            for blk in range(PAIR):
                sent_ref[strided(owner[k] * PAIR + blk, kv)] = piece(k, blk, 3)
                hub = hub + piece(k, blk, 2)
            outside = outside + jnp.where(owner[k] == 0, piece(k, 0, 1), 0.0)
            later = (k + SPLIT - 1) % SPLIT
            own_ref[k, kv, :BLOCK] = piece(k, 0, 0) + piece(k, 1, 1)
            own_ref[k, kv, BLOCK:] = piece(k, 1, 0) + jnp.where(
                owner[later] == 0, 0.0, piece(later, 0, 1)
            )
        sent_ref[strided(HUB, kv)] = hub
        sent_ref[strided(BEFORE, kv)] = outside


def attention(head, kinds, parts, got, logs, deltas):
    tokens = PAIR * BLOCK
    group = (parts[0].shape[0] - 2 * tokens) // (2 * tokens)
    vmem = pl.BlockSpec(memory_space=pltpu.VMEM)
    smem = pl.BlockSpec(memory_space=pltpu.SMEM)
    return pl.pallas_call(
        attend,
        in_specs=[smem, smem] + [vmem] * (SPLIT + 3),
        out_specs=[vmem] * 3,
        out_shape=[
            jax.ShapeDtypeStruct((SPLIT, tokens * group, WIDTH), jnp.bfloat16),
            jax.ShapeDtypeStruct((SPLIT, 2, tokens, WIDTH), jnp.float32),
            jax.ShapeDtypeStruct(got.shape, jnp.float32),
        ],
        scratch_shapes=[pltpu.VMEM(got.shape, jnp.float32)],
        compiler_params=pltpu.CompilerParams(vmem_limit_bytes=VMEM_BYTES),
        cost_estimate=pl.CostEstimate(
            flops=1_400_000_000, bytes_accessed=8_000_000, transcendentals=1_000_000
        ),
    )(head, kinds, *parts, got, logs, deltas)


def pack_back(dq_ref, own_ref, *out_refs):
    rows, tokens = dq_ref.shape[1], own_ref.shape[2]
    for k in range(SPLIT):
        out_refs[k][:rows] = dq_ref[k]
        for kv in range(2):
            total = own_ref[k, kv]
            high = total.astype(jnp.bfloat16)
            low = (total - high.astype(jnp.float32)).astype(jnp.bfloat16)
            start = rows + kv * tokens
            out_refs[k][start : start + tokens] = high
            start = start + 2 * tokens
            out_refs[k][start : start + tokens] = low


def packed_back(dquery, own):
    part = jax.ShapeDtypeStruct((dquery.shape[1] + 4 * own.shape[2], WIDTH), jnp.bfloat16)
    vmem = pl.BlockSpec(memory_space=pltpu.VMEM)
    return pl.pallas_call(
        pack_back,
        in_specs=[vmem] * 2,
        out_specs=[vmem] * SPLIT,
        out_shape=[part] * SPLIT,
        compiler_params=pltpu.CompilerParams(vmem_limit_bytes=VMEM_BYTES),
        cost_estimate=SLOW,
    )(dquery, own)


def unpack(head_ref, *refs):
    parts, (dq_ref, own_ref) = refs[:SPLIT], refs[SPLIT:]
    tokens = dq_ref.shape[0]
    group = dq_ref.shape[1] // SPLIT
    rows = tokens * group
    for k in range(SPLIT):
        for source in range(SPLIT):

            @pl.when(lax.rem(head_ref[0] + k, SPLIT) == source)
            def _(k=k, source=source):
                heads = slice(source * group, (source + 1) * group)
                dq_ref[:, heads, :] = parts[k][:rows].reshape(tokens, group, WIDTH)
                for kv in range(2):
                    start = rows + kv * tokens
                    high = parts[k][start : start + tokens].astype(jnp.float32)
                    start = start + 2 * tokens
                    low = parts[k][start : start + tokens].astype(jnp.float32)
                    own_ref[kv, :, source, :] = high + low


def unpacked(head, parts, queries, keys):
    vmem = pl.BlockSpec(memory_space=pltpu.VMEM)
    return pl.pallas_call(
        unpack,
        in_specs=[pl.BlockSpec(memory_space=pltpu.SMEM)] + [vmem] * SPLIT,
        out_specs=[vmem] * 2,
        out_shape=[
            jax.ShapeDtypeStruct(queries.shape, jnp.bfloat16),
            jax.ShapeDtypeStruct((2,) + keys.shape, jnp.float32),
        ],
        compiler_params=pltpu.CompilerParams(vmem_limit_bytes=VMEM_BYTES),
        cost_estimate=SLOW,
    )(head, *parts)


def finish(home_ref, own_ref, *out_refs):
    rows = own_ref.shape[0] // 2
    half = rows // PAIR
    for kv in range(2):
        for blk in range(PAIR):
            start = blk * half
            total = home_ref[pl.ds(kv * rows + blk, half, stride=PAIR)]
            total = total + own_ref[kv * rows + start : kv * rows + start + half]
            out_refs[kv][start : start + half] = total.astype(jnp.bfloat16)


def finished(home, own):
    out = jax.ShapeDtypeStruct((own.shape[0] // 2, WIDTH), jnp.bfloat16)
    return pl.pallas_call(
        finish,
        out_shape=[out] * 2,
        compiler_params=pltpu.CompilerParams(vmem_limit_bytes=VMEM_BYTES),
    )(home, own)


def pick_rows(index_ref, rows_ref, out_ref):
    blocks = rows_ref.shape[0]
    chunk = 256
    block_at = lax.broadcasted_iota(jnp.int32, (chunk, blocks), 1)
    rows = rows_ref[...]
    for start in range(0, out_ref.shape[0], chunk):
        here = slice(start, start + chunk)
        chosen = jnp.where(block_at == index_ref[here], 1.0, 0.0).astype(jnp.bfloat16)
        out_ref[here] = dot(chosen, rows).astype(jnp.bfloat16)


def gather_rows(index, rows):
    return pl.pallas_call(
        pick_rows,
        out_shape=jax.ShapeDtypeStruct((index.shape[0], WIDTH), jnp.bfloat16),
        compiler_params=pltpu.CompilerParams(vmem_limit_bytes=VMEM_BYTES),
        cost_estimate=pl.CostEstimate(flops=5_000_000_000, bytes_accessed=15_000_000, transcendentals=0),
    )(index, rows)


def add_rows(index_ref, rows_ref, out_ref):
    rows = rows_ref[...]
    high, middle, low = three_parts(rows)
    chunk = 256
    for start in range(0, out_ref.shape[0], chunk):
        block_at = lax.broadcasted_iota(jnp.int32, (chunk, rows.shape[0]), 0) + start
        chosen = jnp.where(block_at == index_ref[...], 1.0, 0.0).astype(jnp.bfloat16)
        out_ref[start : start + chunk] = dot(chosen, high) + dot(chosen, middle) + dot(chosen, low)


def scatter_rows(index, rows, blocks):
    return pl.pallas_call(
        add_rows,
        out_shape=jax.ShapeDtypeStruct((blocks, WIDTH), jnp.float32),
        compiler_params=pltpu.CompilerParams(vmem_limit_bytes=VMEM_BYTES),
    )(index, rows)


def shards(
    queries, key_states, value_states, out_grad, log_sums, row_deltas, block_pairs, pair_kinds
):
    shard_count = lax.axis_size("ctx")
    devices = shard_count * SPLIT
    tokens, key_heads, width = key_states.shape
    heads = queries.shape[1]
    group = heads // key_heads
    blocks = block_pairs.shape[0]
    here = SPLIT * PAIR
    rank, head = lax.axis_index("ctx"), lax.axis_index("head")
    head_at = head.reshape(1)
    wire = (shard_count, SLOTS // 2, 2, width)

    def exchange(array, axes):
        return lax.all_to_all(array, axes, split_axis=0, concat_axis=0, tiled=True)

    pieces = interleaved(key_states.reshape(-1, width), value_states.reshape(-1, width))
    rows = exchange(pieces.reshape(devices, PAIR, width), AXES).reshape(blocks, width)

    far = block_pairs[:, 3].reshape(shard_count, here)
    before = jnp.maximum(here * jnp.arange(shard_count, dtype=jnp.int32) - 1, 0)
    index = jnp.concatenate([far, jnp.zeros_like(before)[:, None], before[:, None]], axis=1)
    kinds = lax.dynamic_slice_in_dim(pair_kinds, rank * here, here, 0)
    later = lax.optimization_barrier((pieces, queries, out_grad, key_states, value_states))
    parts = packed(head_at, *later[1:])
    index, *parts = lax.optimization_barrier((index, *parts))
    got = exchange(gather_rows(index.reshape(-1, 1), rows).reshape(wire), "ctx")

    for k in range(1, SPLIT):
        parts[k] = lax.ppermute(parts[k], "head", [(i, (i + k) % SPLIT) for i in range(SPLIT)])
    log_sums, row_deltas, *parts = lax.optimization_barrier((log_sums, row_deltas, *parts))
    logs, deltas = spread_rows(log_sums, row_deltas)
    dquery, own, sent = attention(head_at, kinds, parts, got.reshape(-1, width), logs, deltas)

    back = exchange(sent.reshape(shard_count, 1, SLOTS * width), "ctx")
    sums = scatter_rows(index.reshape(1, -1), back.reshape(-1, width), blocks)
    home = exchange(sums.reshape(devices, PAIR, width), AXES)

    parts = list(packed_back(dquery, own))
    for k in range(1, SPLIT):
        parts[k] = lax.ppermute(parts[k], "head", [(i, (i - k) % SPLIT) for i in range(SPLIT)])
    dquery, own = unpacked(head_at, parts, queries, key_states)

    dkey, dvalue = finished(home.reshape(-1, width), own.reshape(-1, width))
    return dquery, dkey.reshape(key_states.shape), dvalue.reshape(key_states.shape)


def solution(mesh):
    tokens = P(("ctx", "head"), None, None)
    stats = P("head", "ctx")
    return jax.shard_map(
        shards,
        mesh=mesh,
        in_specs=(tokens, tokens, tokens, tokens, stats, stats, P(), P()),
        out_specs=(tokens, tokens, tokens),
        check_vma=False,
    )
```

```python
import jax
import jax.numpy as jnp
from jax import lax
from jax.experimental import pallas as pl
from jax.experimental.pallas import tpu as pltpu
from jax.sharding import PartitionSpec as P

BLOCK = 64
WIDTH = 128
AXES = ("ctx", "head")
SPLIT = 4
PAIR = 2
SLOTS = SPLIT * PAIR + 2
HUB, BEFORE = SLOTS - 2, SLOTS - 1
VMEM_BYTES = 20 * 1024 * 1024
WHOLE_VMEM = 60 * 1024 * 1024
SLOW = pl.CostEstimate(flops=20_000_000_000, bytes_accessed=60_000_000, transcendentals=0)


def dot(left, right, contract=((1,), (0,))):
    return lax.dot_general(
        left, right, (contract, ((), ())), preferred_element_type=jnp.float32
    )


def three_parts(rows):
    high = rows.astype(jnp.bfloat16)
    rest = rows - high.astype(jnp.float32)
    middle = rest.astype(jnp.bfloat16)
    return high, middle, (rest - middle.astype(jnp.float32)).astype(jnp.bfloat16)


def strided(slot, kv):
    return pl.ds(kv * BLOCK * SLOTS + slot, BLOCK, stride=SLOTS)


def interleave(k_ref, v_ref, pieces_ref, wide_ref):
    half = wide_ref.shape[0] // 4
    for kv, ref in enumerate((k_ref, v_ref)):
        wide = ref[...].astype(jnp.float32)
        for blk in range(PAIR):
            start = 2 * kv * half + blk
            wide_ref[pl.ds(start, half, stride=PAIR)] = wide[blk * half : (blk + 1) * half]
    pieces_ref[...] = wide_ref[...].astype(jnp.bfloat16)


def interleaved(keys, values):
    both = (2 * keys.shape[0], WIDTH)
    return pl.pallas_call(
        interleave,
        out_shape=jax.ShapeDtypeStruct(both, jnp.bfloat16),
        scratch_shapes=[pltpu.VMEM(both, jnp.float32)],
        compiler_params=pltpu.CompilerParams(vmem_limit_bytes=WHOLE_VMEM),
    )(keys, values)


def pack(head_ref, *refs):
    ins, outs, held, (part_ref, in_sems, out_sems) = refs[:4], refs[4:8], refs[8:12], refs[12:]
    tokens = held[0].shape[0]
    group = held[0].shape[1] // SPLIT
    rows = tokens * group
    loads = [pltpu.make_async_copy(ins[i], held[i], in_sems.at[i]) for i in range(4)]
    for load in loads:
        load.start()
    stores = []
    start = 0
    for i, width in enumerate((group, group, 1, 1)):
        here = slice(start, start + tokens * width)
        start = start + tokens * width
        loads[i].wait()
        for k in range(SPLIT):
            for to in range(SPLIT):

                @pl.when(lax.rem(head_ref[0] + k, SPLIT) == to)
                def _(i=i, k=k, to=to, width=width, here=here):
                    heads = slice(to * width, (to + 1) * width)
                    part_ref[k, here] = held[i][:, heads, :].reshape(tokens * width, WIDTH)

            stores.append(
                pltpu.make_async_copy(part_ref.at[k, here], outs[k].at[here], out_sems.at[i, k])
            )
            stores[-1].start()
    for store in stores:
        store.wait()


def packed(head, queries, grads, keys, values):
    tokens, heads, width = queries.shape
    part = (2 * tokens * (heads // SPLIT + 1), width)
    hbm = pl.BlockSpec(memory_space=pltpu.HBM)
    arrays = (queries, grads, keys, values)
    return pl.pallas_call(
        pack,
        in_specs=[pl.BlockSpec(memory_space=pltpu.SMEM)] + [hbm] * 4,
        out_specs=[hbm] * SPLIT,
        out_shape=[jax.ShapeDtypeStruct(part, jnp.bfloat16)] * SPLIT,
        scratch_shapes=[pltpu.VMEM(a.shape, a.dtype) for a in arrays]
        + [
            pltpu.VMEM((SPLIT,) + part, jnp.bfloat16),
            pltpu.SemaphoreType.DMA((4,)),
            pltpu.SemaphoreType.DMA((4, SPLIT)),
        ],
        compiler_params=pltpu.CompilerParams(vmem_limit_bytes=WHOLE_VMEM),
        cost_estimate=SLOW,
    )(head, *arrays)


def spread(*refs):
    stat_refs, row_refs = refs[:2], refs[2:]
    group = stat_refs[0].shape[0]
    columns = BLOCK * group
    stats = jnp.concatenate([ref[...] for ref in stat_refs], axis=0)
    stats = jnp.concatenate(three_parts(stats), axis=0)
    token_at = lax.broadcasted_iota(jnp.int32, (BLOCK, columns), 0)
    column_at = lax.broadcasted_iota(jnp.int32, (BLOCK, columns), 1)
    copies = jnp.where(token_at == column_at // group, 1.0, 0.0).astype(jnp.bfloat16)
    head_at = lax.broadcasted_iota(jnp.int32, (group, columns), 0)
    mine = head_at == lax.broadcasted_iota(jnp.int32, (group, columns), 1) % group
    for at in range(SPLIT * PAIR):
        wide = dot(stats[:, at * BLOCK : (at + 1) * BLOCK], copies)
        for which, row_ref in enumerate(row_refs):
            starts = [(2 * part + which) * group for part in range(3)]
            value = sum(wide[start : start + group] for start in starts)
            row_ref[at] = jnp.sum(jnp.where(mine, value, 0.0), axis=0, keepdims=True)


def spread_rows(*stats):
    vmem = pl.BlockSpec(memory_space=pltpu.VMEM)
    row = jax.ShapeDtypeStruct((SPLIT * PAIR, 1, BLOCK * stats[0].shape[0]), jnp.float32)
    return pl.pallas_call(
        spread,
        in_specs=[vmem] * 2,
        out_specs=[vmem] * 2,
        out_shape=[row, row],
        compiler_params=pltpu.CompilerParams(vmem_limit_bytes=VMEM_BYTES),
        cost_estimate=SLOW,
    )(*stats)


def attend(head_ref, kinds, *refs):
    parts, (got_ref, log_ref, delta_ref), (dq_ref, own_ref, sent_ref) = refs[:4], refs[4:7], refs[7:10]
    wide_ref = refs[10]
    wide_ref[...] = got_ref[...].astype(jnp.float32)
    tokens = PAIR * BLOCK
    group = (parts[0].shape[0] - 2 * tokens) // (2 * tokens)
    rows = BLOCK * group
    scale = WIDTH ** (-0.5)
    key_at = lax.broadcasted_iota(jnp.int32, (BLOCK, rows), 0)
    token_at = lax.broadcasted_iota(jnp.int32, (BLOCK, rows), 1) // group
    causal = key_at <= token_at
    table_at = 2 * tokens * group

    def own(sender, kv, blk):
        start = table_at + kv * tokens + blk * BLOCK
        return parts[sender][start : start + BLOCK]

    def got(slot, kv):
        return wide_ref[strided(slot, kv)].astype(jnp.bfloat16)

    owner = [lax.rem(head_ref[0] + SPLIT - k, SPLIT) for k in range(SPLIT)]
    terms = {}
    for k in range(SPLIT):
        for blk in range(PAIR):
            at = owner[k] * PAIR + blk
            tables = []
            for kv in range(2):
                if blk:
                    before = own(k, kv, 0)
                else:
                    before = jnp.where(owner[k] == 0, got(BEFORE, kv), own((k + 1) % SPLIT, kv, 1))
                tables.append(
                    jnp.concatenate([own(k, kv, blk), before, got(HUB, kv), got(at, kv)], axis=0)
                )
            keys, values = tables
            queries = parts[k][blk * rows : (blk + 1) * rows]
            grads = parts[k][tokens * group + blk * rows : tokens * group + (blk + 1) * rows]
            scores = dot(keys, queries, ((1,), (1,))) * scale
            weights = jnp.exp(scores - log_ref[at])
            masked = [jnp.where(causal, weights[:BLOCK], 0.0)]
            for slot in range(1, 4):
                live = kinds[at, slot] > 0
                masked.append(jnp.where(live, weights[slot * BLOCK : (slot + 1) * BLOCK], 0.0))
            weights = jnp.concatenate(masked, axis=0)
            prob_grad = dot(values, grads, ((1,), (1,)))
            dscore = (weights * (prob_grad - delta_ref[at])).astype(jnp.bfloat16)
            dvalue = dot(weights.astype(jnp.bfloat16), grads)
            dkey = dot(dscore, queries) * scale
            dquery = dot(dscore, keys, ((0,), (0,))) * scale
            dq_ref[k, blk * rows : (blk + 1) * rows] = dquery.astype(jnp.bfloat16)
            terms[k, blk] = (dkey, dvalue)
    for kv in range(2):

        def piece(k, blk, slot):
            return terms[k, blk][kv][slot * BLOCK : (slot + 1) * BLOCK]

        hub = 0.0
        outside = 0.0
        for k in range(SPLIT):
            for blk in range(PAIR):
                sent_ref[strided(owner[k] * PAIR + blk, kv)] = piece(k, blk, 3)
                hub = hub + piece(k, blk, 2)
            outside = outside + jnp.where(owner[k] == 0, piece(k, 0, 1), 0.0)
            later = (k + SPLIT - 1) % SPLIT
            own_ref[k, kv, :BLOCK] = piece(k, 0, 0) + piece(k, 1, 1)
            own_ref[k, kv, BLOCK:] = piece(k, 1, 0) + jnp.where(
                owner[later] == 0, 0.0, piece(later, 0, 1)
            )
        sent_ref[strided(HUB, kv)] = hub
        sent_ref[strided(BEFORE, kv)] = outside


def attention(head, kinds, parts, got, logs, deltas):
    tokens = PAIR * BLOCK
    group = (parts[0].shape[0] - 2 * tokens) // (2 * tokens)
    vmem = pl.BlockSpec(memory_space=pltpu.VMEM)
    smem = pl.BlockSpec(memory_space=pltpu.SMEM)
    return pl.pallas_call(
        attend,
        in_specs=[smem, smem] + [vmem] * (SPLIT + 3),
        out_specs=[vmem] * 3,
        out_shape=[
            jax.ShapeDtypeStruct((SPLIT, tokens * group, WIDTH), jnp.bfloat16),
            jax.ShapeDtypeStruct((SPLIT, 2, tokens, WIDTH), jnp.float32),
            jax.ShapeDtypeStruct(got.shape, jnp.float32),
        ],
        scratch_shapes=[pltpu.VMEM(got.shape, jnp.float32)],
        compiler_params=pltpu.CompilerParams(vmem_limit_bytes=VMEM_BYTES),
        cost_estimate=pl.CostEstimate(
            flops=1_400_000_000, bytes_accessed=8_000_000, transcendentals=1_000_000
        ),
    )(head, kinds, *parts, got, logs, deltas)


def pack_back(dq_ref, own_ref, *out_refs):
    rows, tokens = dq_ref.shape[1], own_ref.shape[2]
    for k in range(SPLIT):
        out_refs[k][:rows] = dq_ref[k]
        for kv in range(2):
            total = own_ref[k, kv]
            high = total.astype(jnp.bfloat16)
            low = (total - high.astype(jnp.float32)).astype(jnp.bfloat16)
            start = rows + kv * tokens
            out_refs[k][start : start + tokens] = high
            start = start + 2 * tokens
            out_refs[k][start : start + tokens] = low


def packed_back(dquery, own):
    part = jax.ShapeDtypeStruct((dquery.shape[1] + 4 * own.shape[2], WIDTH), jnp.bfloat16)
    vmem = pl.BlockSpec(memory_space=pltpu.VMEM)
    return pl.pallas_call(
        pack_back,
        in_specs=[vmem] * 2,
        out_specs=[vmem] * SPLIT,
        out_shape=[part] * SPLIT,
        compiler_params=pltpu.CompilerParams(vmem_limit_bytes=VMEM_BYTES),
        cost_estimate=SLOW,
    )(dquery, own)


def unpack(head_ref, *refs):
    parts, (dq_ref, own_ref) = refs[:SPLIT], refs[SPLIT:]
    tokens = dq_ref.shape[0]
    group = dq_ref.shape[1] // SPLIT
    rows = tokens * group
    for k in range(SPLIT):
        for source in range(SPLIT):

            @pl.when(lax.rem(head_ref[0] + k, SPLIT) == source)
            def _(k=k, source=source):
                heads = slice(source * group, (source + 1) * group)
                dq_ref[:, heads, :] = parts[k][:rows].reshape(tokens, group, WIDTH)
                for kv in range(2):
                    start = rows + kv * tokens
                    high = parts[k][start : start + tokens].astype(jnp.float32)
                    start = start + 2 * tokens
                    low = parts[k][start : start + tokens].astype(jnp.float32)
                    own_ref[kv, :, source, :] = high + low


def unpacked(head, parts, queries, keys):
    vmem = pl.BlockSpec(memory_space=pltpu.VMEM)
    return pl.pallas_call(
        unpack,
        in_specs=[pl.BlockSpec(memory_space=pltpu.SMEM)] + [vmem] * SPLIT,
        out_specs=[vmem] * 2,
        out_shape=[
            jax.ShapeDtypeStruct(queries.shape, jnp.bfloat16),
            jax.ShapeDtypeStruct((2,) + keys.shape, jnp.float32),
        ],
        compiler_params=pltpu.CompilerParams(vmem_limit_bytes=VMEM_BYTES),
        cost_estimate=SLOW,
    )(head, *parts)


def finish(home_ref, own_ref, *out_refs):
    rows = own_ref.shape[0] // 2
    half = rows // PAIR
    for kv in range(2):
        for blk in range(PAIR):
            start = blk * half
            total = home_ref[pl.ds(kv * rows + blk, half, stride=PAIR)]
            total = total + own_ref[kv * rows + start : kv * rows + start + half]
            out_refs[kv][start : start + half] = total.astype(jnp.bfloat16)


def finished(home, own):
    out = jax.ShapeDtypeStruct((own.shape[0] // 2, WIDTH), jnp.bfloat16)
    return pl.pallas_call(
        finish,
        out_shape=[out] * 2,
        compiler_params=pltpu.CompilerParams(vmem_limit_bytes=VMEM_BYTES),
    )(home, own)


def pick_rows(pairs_ref, rows_ref, out_ref, all_ref, far_ref, wide_ref):
    blocks = rows_ref.shape[0]
    here = SPLIT * PAIR
    askers = blocks // here
    rows = rows_ref[...]
    all_ref[...] = rows.astype(jnp.float32)
    chunk = 256
    block_at = lax.broadcasted_iota(jnp.int32, (blocks, chunk), 0)
    for start in range(0, blocks, chunk):
        chosen = jnp.where(block_at == pairs_ref[3:4, start : start + chunk], 1.0, 0.0)
        far = dot(rows, chosen.astype(jnp.bfloat16), ((0,), (0,)))
        far_ref[start : start + chunk] = far.T
    for slot in range(here):
        wide_ref[pl.ds(slot, askers, stride=SLOTS)] = far_ref[pl.ds(slot, askers, stride=here)]
    first = all_ref[:1]
    wide_ref[pl.ds(HUB, askers, stride=SLOTS)] = jnp.broadcast_to(first, (askers, WIDTH))
    wide_ref[BEFORE : BEFORE + 1] = first
    wide_ref[pl.ds(SLOTS + BEFORE, askers, stride=SLOTS)] = all_ref[pl.ds(here - 1, askers, stride=here)]
    out_ref[...] = wide_ref[: askers * SLOTS].astype(jnp.bfloat16)


def gather_rows(pairs, rows):
    blocks = rows.shape[0]
    asked = blocks // (SPLIT * PAIR) * SLOTS
    return pl.pallas_call(
        pick_rows,
        out_shape=jax.ShapeDtypeStruct((asked, WIDTH), jnp.bfloat16),
        scratch_shapes=[
            pltpu.VMEM((blocks, WIDTH), jnp.float32),
            pltpu.VMEM((blocks, WIDTH), jnp.float32),
            pltpu.VMEM((asked + 16, WIDTH), jnp.float32),
        ],
        compiler_params=pltpu.CompilerParams(vmem_limit_bytes=VMEM_BYTES),
        cost_estimate=pl.CostEstimate(
            flops=5_000_000_000, bytes_accessed=15_000_000, transcendentals=0
        ),
    )(pairs, rows)


def add_rows(pairs_ref, rows_ref, out_ref, far_ref, shift_ref):
    blocks = out_ref.shape[0]
    here = SPLIT * PAIR
    askers = blocks // here
    for slot in range(here):
        far_ref[pl.ds(slot, askers, stride=here)] = rows_ref[pl.ds(slot, askers, stride=SLOTS)]
    high, middle, low = three_parts(far_ref[...])
    hub = jnp.sum(rows_ref[pl.ds(HUB, askers, stride=SLOTS)], axis=0, keepdims=True)
    chunk = 256
    for start in range(0, blocks, chunk):
        block_at = lax.broadcasted_iota(jnp.int32, (chunk, blocks), 0) + start
        chosen = jnp.where(block_at == pairs_ref[3:4, :], 1.0, 0.0).astype(jnp.bfloat16)
        out_ref[start : start + chunk] = dot(chosen, high) + dot(chosen, middle) + dot(chosen, low)
    out_ref[:1] = out_ref[:1] + hub
    shift_ref[:askers] = rows_ref[pl.ds(BEFORE, askers, stride=SLOTS)]
    shift_ref[askers:] = jnp.zeros((8, WIDTH), jnp.float32)
    last = pl.ds(here - 1, askers, stride=here)
    out_ref[last] = out_ref[last] + shift_ref[1 : askers + 1]


def scatter_rows(pairs, rows, blocks):
    askers = blocks // (SPLIT * PAIR)
    return pl.pallas_call(
        add_rows,
        out_shape=jax.ShapeDtypeStruct((blocks, WIDTH), jnp.float32),
        scratch_shapes=[
            pltpu.VMEM((blocks, WIDTH), jnp.float32),
            pltpu.VMEM((askers + 8, WIDTH), jnp.float32),
        ],
        compiler_params=pltpu.CompilerParams(vmem_limit_bytes=VMEM_BYTES),
    )(pairs, rows)


def shards(
    queries, key_states, value_states, out_grad, log_sums, row_deltas, block_pairs, pair_kinds
):
    shard_count = lax.axis_size("ctx")
    devices = shard_count * SPLIT
    tokens, key_heads, width = key_states.shape
    heads = queries.shape[1]
    group = heads // key_heads
    blocks = block_pairs.shape[0]
    here = SPLIT * PAIR
    rank, head = lax.axis_index("ctx"), lax.axis_index("head")
    head_at = head.reshape(1)
    wire = (shard_count, SLOTS // 2, 2, width)

    def exchange(array, axes):
        return lax.all_to_all(array, axes, split_axis=0, concat_axis=0, tiled=True)

    pieces = interleaved(key_states.reshape(-1, width), value_states.reshape(-1, width))
    rows = exchange(pieces.reshape(devices, PAIR, width), AXES).reshape(blocks, width)

    kinds = lax.dynamic_slice_in_dim(pair_kinds, rank * here, here, 0)
    later = lax.optimization_barrier((pieces, queries, out_grad, key_states, value_states))
    parts = packed(head_at, *later[1:])
    pairs, *parts = lax.optimization_barrier((block_pairs.T, *parts))
    got = exchange(gather_rows(pairs, rows).reshape(wire), "ctx")

    for k in range(1, SPLIT):
        parts[k] = lax.ppermute(parts[k], "head", [(i, (i + k) % SPLIT) for i in range(SPLIT)])
    log_sums, row_deltas, *parts = lax.optimization_barrier((log_sums, row_deltas, *parts))
    logs, deltas = spread_rows(log_sums, row_deltas)
    dquery, own, sent = attention(head_at, kinds, parts, got.reshape(-1, width), logs, deltas)

    back = exchange(sent.reshape(shard_count, 1, SLOTS * width), "ctx")
    sums = scatter_rows(pairs, back.reshape(-1, width), blocks)
    home = exchange(sums.reshape(devices, PAIR, width), AXES)

    parts = list(packed_back(dquery, own))
    for k in range(1, SPLIT):
        parts[k] = lax.ppermute(parts[k], "head", [(i, (i - k) % SPLIT) for i in range(SPLIT)])
    dquery, own = unpacked(head_at, parts, queries, key_states)

    dkey, dvalue = finished(home.reshape(-1, width), own.reshape(-1, width))
    return dquery, dkey.reshape(key_states.shape), dvalue.reshape(key_states.shape)


def solution(mesh):
    tokens = P(("ctx", "head"), None, None)
    stats = P("head", "ctx")
    return jax.shard_map(
        shards,
        mesh=mesh,
        in_specs=(tokens, tokens, tokens, tokens, stats, stats, P(), P()),
        out_specs=(tokens, tokens, tokens),
        check_vma=False,
    )
```

```python
import jax
import jax.numpy as jnp
from jax import lax
from jax.experimental import pallas as pl
from jax.experimental.pallas import tpu as pltpu
from jax.sharding import PartitionSpec as P

BLOCK = 64
WIDTH = 128
AXES = ("ctx", "head")
SPLIT = 4
PAIR = 2
SLOTS = SPLIT * PAIR + 2
HUB, BEFORE = SLOTS - 2, SLOTS - 1
SPARE = 16
VMEM_BYTES = 20 * 1024 * 1024
WHOLE_VMEM = 60 * 1024 * 1024
SLOW = pl.CostEstimate(flops=20_000_000_000, bytes_accessed=60_000_000, transcendentals=0)


def dot(left, right, contract=((1,), (0,))):
    return lax.dot_general(
        left, right, (contract, ((), ())), preferred_element_type=jnp.float32
    )


def three_parts(rows):
    high = rows.astype(jnp.bfloat16)
    rest = rows - high.astype(jnp.float32)
    middle = rest.astype(jnp.bfloat16)
    return high, middle, (rest - middle.astype(jnp.float32)).astype(jnp.bfloat16)


def strided(slot, kv):
    return pl.ds(kv * BLOCK * SLOTS + slot, BLOCK, stride=SLOTS)


def interleave(k_ref, v_ref, pieces_ref, wide_ref):
    half = pieces_ref.shape[0] // 4
    for kv, ref in enumerate((k_ref, v_ref)):
        wide = ref[...].astype(jnp.float32)
        for blk in range(PAIR):
            start = 2 * kv * half + blk
            wide_ref[pl.ds(start, half, stride=PAIR)] = wide[blk * half : (blk + 1) * half]
    pieces_ref[...] = wide_ref[: pieces_ref.shape[0]].astype(jnp.bfloat16)


def interleaved(keys, values):
    both = (2 * keys.shape[0], WIDTH)
    return pl.pallas_call(
        interleave,
        out_shape=jax.ShapeDtypeStruct(both, jnp.bfloat16),
        scratch_shapes=[pltpu.VMEM((both[0] + SPARE, WIDTH), jnp.float32)],
        compiler_params=pltpu.CompilerParams(vmem_limit_bytes=WHOLE_VMEM),
    )(keys, values)


def pack(head_ref, *refs):
    ins, outs, held, (part_ref, in_sems, out_sems) = refs[:4], refs[4:8], refs[8:12], refs[12:]
    tokens = held[0].shape[0]
    group = held[0].shape[1] // SPLIT
    rows = tokens * group
    loads = [pltpu.make_async_copy(ins[i], held[i], in_sems.at[i]) for i in range(4)]
    for load in loads:
        load.start()
    stores = []
    start = 0
    for i, width in enumerate((group, group, 1, 1)):
        here = slice(start, start + tokens * width)
        start = start + tokens * width
        loads[i].wait()
        for head in range(SPLIT):

            @pl.when(head_ref[0] == head)
            def _(i=i, head=head, width=width, here=here):
                whole = held[i][...]
                for k in range(SPLIT):
                    to = (head + k) % SPLIT
                    part = whole[:, to * width : (to + 1) * width, :]
                    part_ref[k, here] = part.reshape(tokens * width, WIDTH)

        for k in range(SPLIT):
            stores.append(
                pltpu.make_async_copy(part_ref.at[k, here], outs[k].at[here], out_sems.at[i, k])
            )
            stores[-1].start()
    for store in stores:
        store.wait()


def packed(head, queries, grads, keys, values):
    tokens, heads, width = queries.shape
    part = (2 * tokens * (heads // SPLIT + 1), width)
    hbm = pl.BlockSpec(memory_space=pltpu.HBM)
    arrays = (queries, grads, keys, values)
    return pl.pallas_call(
        pack,
        in_specs=[pl.BlockSpec(memory_space=pltpu.SMEM)] + [hbm] * 4,
        out_specs=[hbm] * SPLIT,
        out_shape=[jax.ShapeDtypeStruct(part, jnp.bfloat16)] * SPLIT,
        scratch_shapes=[pltpu.VMEM(a.shape, a.dtype) for a in arrays]
        + [
            pltpu.VMEM((SPLIT,) + part, jnp.bfloat16),
            pltpu.SemaphoreType.DMA((4,)),
            pltpu.SemaphoreType.DMA((4, SPLIT)),
        ],
        compiler_params=pltpu.CompilerParams(vmem_limit_bytes=WHOLE_VMEM),
        cost_estimate=SLOW,
    )(head, *arrays)


def spread(*refs):
    stat_refs, row_refs = refs[:2], refs[2:]
    group = stat_refs[0].shape[0]
    columns = BLOCK * group
    stats = jnp.concatenate([ref[...] for ref in stat_refs], axis=0)
    stats = jnp.concatenate(three_parts(stats), axis=0)
    token_at = lax.broadcasted_iota(jnp.int32, (BLOCK, columns), 0)
    column_at = lax.broadcasted_iota(jnp.int32, (BLOCK, columns), 1)
    copies = jnp.where(token_at == column_at // group, 1.0, 0.0).astype(jnp.bfloat16)
    head_at = lax.broadcasted_iota(jnp.int32, (group, columns), 0)
    mine = head_at == lax.broadcasted_iota(jnp.int32, (group, columns), 1) % group
    for at in range(SPLIT * PAIR):
        wide = dot(stats[:, at * BLOCK : (at + 1) * BLOCK], copies)
        for which, row_ref in enumerate(row_refs):
            starts = [(2 * part + which) * group for part in range(3)]
            value = sum(wide[start : start + group] for start in starts)
            row_ref[at] = jnp.sum(jnp.where(mine, value, 0.0), axis=0, keepdims=True)


def spread_rows(*stats):
    vmem = pl.BlockSpec(memory_space=pltpu.VMEM)
    row = jax.ShapeDtypeStruct((SPLIT * PAIR, 1, BLOCK * stats[0].shape[0]), jnp.float32)
    return pl.pallas_call(
        spread,
        in_specs=[vmem] * 2,
        out_specs=[vmem] * 2,
        out_shape=[row, row],
        compiler_params=pltpu.CompilerParams(vmem_limit_bytes=VMEM_BYTES),
        cost_estimate=SLOW,
    )(*stats)


def attend(head_ref, kinds, *refs):
    parts, (got_ref, log_ref, delta_ref), (*backs, sent_ref) = refs[:4], refs[4:7], refs[7:12]
    wide_ref, held_ref = refs[12:]
    wide_ref[: got_ref.shape[0]] = got_ref[...].astype(jnp.float32)
    tokens = PAIR * BLOCK
    group = (parts[0].shape[0] - 2 * tokens) // (2 * tokens)
    rows = BLOCK * group
    scale = WIDTH ** (-0.5)
    key_at = lax.broadcasted_iota(jnp.int32, (BLOCK, rows), 0)
    token_at = lax.broadcasted_iota(jnp.int32, (BLOCK, rows), 1) // group
    causal = key_at <= token_at
    table_at = 2 * tokens * group

    def own(sender, kv, blk):
        start = table_at + kv * tokens + blk * BLOCK
        return parts[sender][start : start + BLOCK]

    def got(slot, kv):
        return wide_ref[strided(slot, kv)].astype(jnp.bfloat16)

    owner = [lax.rem(head_ref[0] + SPLIT - k, SPLIT) for k in range(SPLIT)]
    terms = {}
    for k in range(SPLIT):
        for blk in range(PAIR):
            at = owner[k] * PAIR + blk
            tables = []
            for kv in range(2):
                if blk:
                    before = own(k, kv, 0)
                else:
                    before = jnp.where(owner[k] == 0, got(BEFORE, kv), own((k + 1) % SPLIT, kv, 1))
                tables.append(
                    jnp.concatenate([own(k, kv, blk), before, got(HUB, kv), got(at, kv)], axis=0)
                )
            keys, values = tables
            queries = parts[k][blk * rows : (blk + 1) * rows]
            grads = parts[k][tokens * group + blk * rows : tokens * group + (blk + 1) * rows]
            scores = dot(keys, queries, ((1,), (1,))) * scale
            weights = jnp.exp(scores - log_ref[at])
            masked = [jnp.where(causal, weights[:BLOCK], 0.0)]
            for slot in range(1, 4):
                live = kinds[at, slot] > 0
                masked.append(jnp.where(live, weights[slot * BLOCK : (slot + 1) * BLOCK], 0.0))
            weights = jnp.concatenate(masked, axis=0)
            prob_grad = dot(values, grads, ((1,), (1,)))
            dscore = (weights * (prob_grad - delta_ref[at])).astype(jnp.bfloat16)
            dvalue = dot(weights.astype(jnp.bfloat16), grads)
            dkey = dot(dscore, queries) * scale
            dquery = dot(dscore, keys, ((0,), (0,))) * scale
            backs[k][blk * rows : (blk + 1) * rows] = dquery.astype(jnp.bfloat16)
            terms[k, blk] = (dkey, dvalue)
    for kv in range(2):

        def piece(k, blk, slot):
            return terms[k, blk][kv][slot * BLOCK : (slot + 1) * BLOCK]

        hub = 0.0
        outside = 0.0
        for k in range(SPLIT):
            for blk in range(PAIR):
                held_ref[strided(owner[k] * PAIR + blk, kv)] = piece(k, blk, 3)
                hub = hub + piece(k, blk, 2)
            outside = outside + jnp.where(owner[k] == 0, piece(k, 0, 1), 0.0)
            later = (k + SPLIT - 1) % SPLIT
            first = piece(k, 0, 0) + piece(k, 1, 1)
            second = piece(k, 1, 0) + jnp.where(owner[later] == 0, 0.0, piece(later, 0, 1))
            for blk, total in enumerate((first, second)):
                high = total.astype(jnp.bfloat16)
                low = (total - high.astype(jnp.float32)).astype(jnp.bfloat16)
                start = tokens * group + kv * tokens + blk * BLOCK
                backs[k][start : start + BLOCK] = high
                start = start + 2 * tokens
                backs[k][start : start + BLOCK] = low
        held_ref[strided(HUB, kv)] = hub
        held_ref[strided(BEFORE, kv)] = outside
    sent_ref[...] = held_ref[: sent_ref.shape[0]]


def attention(head, kinds, parts, got, logs, deltas):
    tokens = PAIR * BLOCK
    group = (parts[0].shape[0] - 2 * tokens) // (2 * tokens)
    vmem = pl.BlockSpec(memory_space=pltpu.VMEM)
    smem = pl.BlockSpec(memory_space=pltpu.SMEM)
    return pl.pallas_call(
        attend,
        in_specs=[smem, smem] + [vmem] * (SPLIT + 3),
        out_specs=[vmem] * (SPLIT + 1),
        out_shape=[jax.ShapeDtypeStruct((tokens * group + 4 * tokens, WIDTH), jnp.bfloat16)] * SPLIT
        + [jax.ShapeDtypeStruct(got.shape, jnp.float32)],
        scratch_shapes=[pltpu.VMEM((got.shape[0] + SPARE, WIDTH), jnp.float32)] * 2,
        compiler_params=pltpu.CompilerParams(vmem_limit_bytes=VMEM_BYTES),
        cost_estimate=pl.CostEstimate(
            flops=1_400_000_000, bytes_accessed=8_000_000, transcendentals=1_000_000
        ),
    )(head, kinds, *parts, got, logs, deltas)


def unpack(head_ref, *refs):
    parts, (dq_ref, own_ref) = refs[:SPLIT], refs[SPLIT:]
    tokens = dq_ref.shape[0]
    group = dq_ref.shape[1] // SPLIT
    rows = tokens * group
    for head in range(SPLIT):

        @pl.when(head_ref[0] == head)
        def _(head=head):
            senders = [parts[(source - head) % SPLIT] for source in range(SPLIT)]
            for source in range(0, SPLIT, 2):
                pair = [senders[source + i][:rows].reshape(tokens, group, WIDTH) for i in range(2)]
                heads = slice(source * group, (source + 2) * group)
                dq_ref[:, heads, :] = jnp.concatenate(pair, axis=1)
            for source, sender in enumerate(senders):
                for kv in range(2):
                    start = rows + kv * tokens
                    high = sender[start : start + tokens].astype(jnp.float32)
                    start = start + 2 * tokens
                    low = sender[start : start + tokens].astype(jnp.float32)
                    own_ref[kv, :, source, :] = high + low


def unpacked(head, parts, queries, keys):
    vmem = pl.BlockSpec(memory_space=pltpu.VMEM)
    return pl.pallas_call(
        unpack,
        in_specs=[pl.BlockSpec(memory_space=pltpu.SMEM)] + [vmem] * SPLIT,
        out_specs=[vmem] * 2,
        out_shape=[
            jax.ShapeDtypeStruct(queries.shape, jnp.bfloat16),
            jax.ShapeDtypeStruct((2,) + keys.shape, jnp.float32),
        ],
        compiler_params=pltpu.CompilerParams(vmem_limit_bytes=VMEM_BYTES),
        cost_estimate=SLOW,
    )(head, *parts)


def finish(home_ref, own_ref, *out_refs):
    rows = own_ref.shape[0] // 2
    half = rows // PAIR
    for kv in range(2):
        for blk in range(PAIR):
            start = blk * half
            total = home_ref[pl.ds(kv * rows + blk, half, stride=PAIR)]
            total = total + own_ref[kv * rows + start : kv * rows + start + half]
            out_refs[kv][start : start + half] = total.astype(jnp.bfloat16)


def finished(home, own):
    out = jax.ShapeDtypeStruct((own.shape[0] // 2, WIDTH), jnp.bfloat16)
    return pl.pallas_call(
        finish,
        out_shape=[out] * 2,
        compiler_params=pltpu.CompilerParams(vmem_limit_bytes=VMEM_BYTES),
    )(home, own)


def pick_rows(pairs_ref, rows_ref, out_ref, all_ref, far_ref, wide_ref):
    blocks = rows_ref.shape[0]
    here = SPLIT * PAIR
    askers = blocks // here
    rows = rows_ref[...]
    all_ref[:blocks] = rows.astype(jnp.float32)
    chunk = 256
    block_at = lax.broadcasted_iota(jnp.int32, (blocks, chunk), 0)
    for start in range(0, blocks, chunk):
        chosen = jnp.where(block_at == pairs_ref[3:4, start : start + chunk], 1.0, 0.0)
        far = dot(rows, chosen.astype(jnp.bfloat16), ((0,), (0,)))
        far_ref[start : start + chunk] = far.T
    for slot in range(here):
        wide_ref[pl.ds(slot, askers, stride=SLOTS)] = far_ref[pl.ds(slot, askers, stride=here)]
    first = all_ref[:1]
    wide_ref[pl.ds(HUB, askers, stride=SLOTS)] = jnp.broadcast_to(first, (askers, WIDTH))
    wide_ref[BEFORE : BEFORE + 1] = first
    wide_ref[pl.ds(SLOTS + BEFORE, askers, stride=SLOTS)] = all_ref[pl.ds(here - 1, askers, stride=here)]
    out_ref[...] = wide_ref[: askers * SLOTS].astype(jnp.bfloat16)


def gather_rows(pairs, rows):
    blocks = rows.shape[0]
    asked = blocks // (SPLIT * PAIR) * SLOTS
    return pl.pallas_call(
        pick_rows,
        out_shape=jax.ShapeDtypeStruct((asked, WIDTH), jnp.bfloat16),
        scratch_shapes=[
            pltpu.VMEM((blocks + SPARE, WIDTH), jnp.float32),
            pltpu.VMEM((blocks + SPARE, WIDTH), jnp.float32),
            pltpu.VMEM((asked + 2 * SPARE, WIDTH), jnp.float32),
        ],
        compiler_params=pltpu.CompilerParams(vmem_limit_bytes=VMEM_BYTES),
        cost_estimate=pl.CostEstimate(
            flops=5_000_000_000, bytes_accessed=15_000_000, transcendentals=0
        ),
    )(pairs, rows)


def mark(pairs_ref, out_ref):
    blocks = out_ref.shape[0]
    chunk = 256
    for start in range(0, blocks, chunk):
        block_at = lax.broadcasted_iota(jnp.int32, (chunk, blocks), 0) + start
        chosen = jnp.where(block_at == pairs_ref[3:4, :], 1.0, 0.0)
        out_ref[start : start + chunk] = chosen.astype(jnp.bfloat16)


def marked(pairs):
    return pl.pallas_call(
        mark,
        out_shape=jax.ShapeDtypeStruct((pairs.shape[1], pairs.shape[1]), jnp.bfloat16),
        compiler_params=pltpu.CompilerParams(vmem_limit_bytes=VMEM_BYTES),
        cost_estimate=SLOW,
    )(pairs)


def add_rows(chosen_ref, rows_ref, out_ref, far_ref, shift_ref):
    blocks = out_ref.shape[0]
    here = SPLIT * PAIR
    askers = blocks // here
    for slot in range(here):
        far_ref[pl.ds(slot, askers, stride=here)] = rows_ref[pl.ds(slot, askers, stride=SLOTS)]
    parts = jnp.concatenate(three_parts(far_ref[:blocks]), axis=1)
    hub = jnp.sum(rows_ref[pl.ds(HUB, askers, stride=SLOTS)], axis=0, keepdims=True)
    sums = dot(chosen_ref[...], parts)
    out_ref[...] = sums[:, :WIDTH] + sums[:, WIDTH : 2 * WIDTH] + sums[:, 2 * WIDTH :]
    out_ref[:1] = out_ref[:1] + hub
    shift_ref[:askers] = rows_ref[pl.ds(BEFORE, askers, stride=SLOTS)]
    shift_ref[askers:] = jnp.zeros((8, WIDTH), jnp.float32)
    last = pl.ds(here - 1, askers, stride=here)
    out_ref[last] = out_ref[last] + shift_ref[1 : askers + 1]


def scatter_rows(chosen, rows, blocks):
    askers = blocks // (SPLIT * PAIR)
    return pl.pallas_call(
        add_rows,
        out_shape=jax.ShapeDtypeStruct((blocks, WIDTH), jnp.float32),
        scratch_shapes=[
            pltpu.VMEM((blocks + SPARE, WIDTH), jnp.float32),
            pltpu.VMEM((askers + 8, WIDTH), jnp.float32),
        ],
        compiler_params=pltpu.CompilerParams(vmem_limit_bytes=VMEM_BYTES),
    )(chosen, rows)


def shards(
    queries, key_states, value_states, out_grad, log_sums, row_deltas, block_pairs, pair_kinds
):
    shard_count = lax.axis_size("ctx")
    devices = shard_count * SPLIT
    tokens, key_heads, width = key_states.shape
    heads = queries.shape[1]
    group = heads // key_heads
    blocks = block_pairs.shape[0]
    here = SPLIT * PAIR
    rank, head = lax.axis_index("ctx"), lax.axis_index("head")
    head_at = head.reshape(1)
    wire = (shard_count, SLOTS // 2, 2, width)

    def exchange(array, axes):
        return lax.all_to_all(array, axes, split_axis=0, concat_axis=0, tiled=True)

    pieces = interleaved(key_states.reshape(-1, width), value_states.reshape(-1, width))
    rows = exchange(pieces.reshape(devices, PAIR, width), AXES).reshape(blocks, width)

    kinds = lax.dynamic_slice_in_dim(pair_kinds, rank * here, here, 0)
    later = lax.optimization_barrier((pieces, queries, out_grad, key_states, value_states))
    parts = packed(head_at, *later[1:])
    pairs, *parts = lax.optimization_barrier((block_pairs.T, *parts))
    got = exchange(gather_rows(pairs, rows).reshape(wire), "ctx")

    for k in (2, 1, 3):
        parts[k] = lax.ppermute(parts[k], "head", [(i, (i + k) % SPLIT) for i in range(SPLIT)])
    log_sums, row_deltas, *parts = lax.optimization_barrier((log_sums, row_deltas, *parts))
    logs, deltas = spread_rows(log_sums, row_deltas)
    *parts, sent = attention(head_at, kinds, parts, got.reshape(-1, width), logs, deltas)

    back = exchange(sent.reshape(shard_count, 1, SLOTS * width), "ctx")
    pairs, parts[0] = lax.optimization_barrier((pairs, parts[0]))
    sums = scatter_rows(marked(pairs), back.reshape(-1, width), blocks)
    home = exchange(sums.reshape(devices, PAIR, width), AXES)

    for k in range(1, SPLIT):
        parts[k] = lax.ppermute(parts[k], "head", [(i, (i - k) % SPLIT) for i in range(SPLIT)])
    dquery, own = unpacked(head_at, parts, queries, key_states)

    dkey, dvalue = finished(home.reshape(-1, width), own.reshape(-1, width))
    return dquery, dkey.reshape(key_states.shape), dvalue.reshape(key_states.shape)


def solution(mesh):
    tokens = P(("ctx", "head"), None, None)
    stats = P("head", "ctx")
    return jax.shard_map(
        shards,
        mesh=mesh,
        in_specs=(tokens, tokens, tokens, tokens, stats, stats, P(), P()),
        out_specs=(tokens, tokens, tokens),
        check_vma=False,
    )
```
